512 devices in a mesh: walker: 128 (over z, y, core), space: 4 (over x).
Axes of the slice: x: 4, y: 8, z: 8, core: 2. Of those that a mesh axis runs over, the one named last changes fastest.
Arguments:
- positions: float32 [128, 3, 12288], P('walker', None, 'space'), may hold values from -6 to 6
- velocities: float32 [128, 3, 12288], P('walker', None, 'space'), may hold values from -6 to 6
- weights: float32 [128], P('walker'), may hold values from 0.2 to 2
- strength: float32 [12288], P('space'), may hold values from 0.3 to 3
- tiles: int32 [96, 27], P('space'), may hold values from 0 to 27, as said below
- plan: int32 [128], replicated, may hold values from 0 to 127
- home: int32 [128], replicated, may hold values from 0 to 127, as said below
Outputs:
- distances: float32 [128, 128], P('walker', 'space')
- new_positions: float32 [128, 3, 12288], P('walker', None, 'space')
- new_velocities: float32 [128, 3, 12288], P('walker', None, 'space')
- new_weights: float32 [128], P('walker')
The draws below stay inside these ranges and needn't reach their ends.
Inputs may be any that keep to these rules, and one draw needn't show every extreme that they name: tiles[g, k] - 2 + (g // 24) * 24 is a cell inside the walker's grid at most 2 cells from g; entries 1 and 2 of each list are the cells 2 before and 2 after g, or the nearest end cell where those do not exist; entries may repeat. home is a permutation.
All inputs are finite; a program needn't handle non-finite values.
Results may differ from the reference program's by a relative error of at most 0.0003.
Values may be sent and summed in bfloat16 or wider, within the bound.
A program may use at most 64 MiB of HBM per device.

```python
import math
import jax
import jax.numpy as jnp
from jax import lax

CELLS = 24
TILE = 128
NBR = 27
HALO = 2
SITES = 8192
WALKERS = 128
NCELLS = 96
ATOMS_DEV = 3072
ATOMS = 12288
SITE_DEV = 2048
N_SPACE = 4


def draw_tiles(key, part):
    key = jax.random.fold_in(key, 7)
    cell_ids = jnp.arange(NCELLS, dtype=jnp.int32)
    offsets = jax.random.randint(key, (NCELLS, NBR), -HALO, HALO + 1, dtype=jnp.int32)
    lower = jnp.full((NCELLS, 1), -HALO, jnp.int32)
    upper = jnp.full((NCELLS, 1), HALO, jnp.int32)
    offsets = jnp.concatenate([offsets[:, :1], lower, upper, offsets[:, 3:]], axis=1)
    target = jnp.clip(cell_ids[:, None] + offsets, 0, NCELLS - 1)
    return (target - (cell_ids // CELLS * CELLS)[:, None] + HALO).astype(jnp.int32)


def home_rows(key):
    return jax.random.permutation(jax.random.fold_in(key, 101), WALKERS).astype(jnp.int32)


def draw_home(key, part):
    return home_rows(key)


def draw_plan(key, part):
    rows = home_rows(key)
    key = jax.random.fold_in(key, 11)
    first, second, third, fourth = jax.random.split(key, 4)
    labels = jnp.arange(WALKERS, dtype=jnp.int32)
    inverse = jnp.zeros((WALKERS,), jnp.int32).at[rows].set(labels)
    order = jax.random.permutation(first, WALKERS).astype(jnp.int32)
    left = jax.random.randint(second, (WALKERS,), 0, WALKERS, dtype=jnp.int32)
    right = jax.random.randint(third, (WALKERS,), 0, WALKERS, dtype=jnp.int32)
    chosen = order[jnp.minimum(left, right)]
    start = jax.random.randint(fourth, (), 0, WALKERS, dtype=jnp.int32)
    quarter = WALKERS // 4
    slot_a = start % WALKERS
    slot_b = (start + quarter) % WALKERS
    slot_c = (start + 2 * quarter) % WALKERS
    slot_d = (start + 3 * quarter) % WALKERS
    chosen = chosen.at[slot_a].set(inverse[(slot_a + WALKERS - 1) % WALKERS])
    chosen = chosen.at[slot_b].set(inverse[(slot_b + WALKERS // 2) % WALKERS])
    chosen = chosen.at[slot_c].set(jnp.int32(0))
    chosen = chosen.at[slot_d].set(jnp.int32(WALKERS - 1))
    return chosen.astype(jnp.int32)


def steps_of(own_key, shape, cuts, least, top_value):
    factor_of = 1.0
    for position, blocks in cuts:
        draws = jax.random.uniform(jax.random.fold_in(jax.random.fold_in(own_key, 6), position), (blocks,), jnp.float32, least / len(cuts), top_value / len(cuts))
        factor_of = factor_of * jnp.repeat(jnp.exp(draws), shape[position] // blocks).reshape((-1,) + (1,) * (len(shape) - 1 - position))
    return factor_of


def noise(key, shape, width, limit, shards=(), kind=jnp.bfloat16):
    values = width * jax.random.normal(key, shape, jnp.float32)
    if shards:
        values = values * steps_of(key, shape, shards, -0.22, 0.18)
    return jnp.clip(values, -limit, limit).astype(kind)


def setup_inputs(seed: int = 0) -> dict:
    streams_of = jax.random.split(jax.random.key(seed), 8)
    return {
        "positions": noise(streams_of[0], (WALKERS, 3, ATOMS), 1.0, 6.0, ((0, 128), (2, 4)), jnp.float32),
        "velocities": noise(streams_of[1], (WALKERS, 3, ATOMS), 1.0, 6.0, ((0, 128), (2, 4)), jnp.float32),
        "weights": jnp.clip(jnp.exp(math.log(2.0) - 2.3025851 * jax.random.uniform(streams_of[2], (WALKERS,), jnp.float32) ** steps_of(streams_of[2], (WALKERS,), ((0, 128),), -0.2, 0.2)), 0.2, 2.0),
        "strength": jnp.clip(jnp.exp(math.log(3.0) - 2.3025851 * jax.random.uniform(streams_of[3], (ATOMS,), jnp.float32) ** steps_of(streams_of[3], (ATOMS,), ((0, 4),), -0.2, 0.2)), 0.3, 3.0),
        "tiles": draw_tiles(jax.random.fold_in(streams_of[7], 71), 0),
        "plan": draw_plan(jax.random.fold_in(streams_of[7], 71), 0),
        "home": draw_home(jax.random.fold_in(streams_of[7], 71), 0),
    }


STEP = 0.1


def tile_force(pos, near, near_str):
    delta = pos[..., :, None] - near[..., None, :]
    radius = jnp.sum(delta * delta, axis=1)
    factor = near_str[:, None, :] / jnp.square(1.0 + radius)
    return jnp.sum(factor[:, None] * delta, axis=-1)


def forces(pos, ext_pos, ext_str, str_loc, table):
    def turn(k, total):
        column = lax.dynamic_index_in_dim(table, k, 1, keepdims=False)
        near = jnp.take(ext_pos, column, axis=2)
        near_str = jnp.take(ext_str, column, axis=0)
        return total + tile_force(pos, near, near_str)

    total = lax.fori_loop(0, NBR, turn, jnp.zeros(pos.shape, jnp.float32))
    return str_loc * total


def reference(positions, velocities, weights, strength, tiles, plan, home):
    cell_ids = jnp.arange(NCELLS, dtype=jnp.int32)
    global_cells = (cell_ids // CELLS * CELLS)[:, None] + tiles - HALO
    str_cells = strength.reshape(NCELLS, TILE)

    def walk(state):
        pos = state[0].reshape(1, 3, NCELLS, TILE)
        vel = state[1].reshape(1, 3, NCELLS, TILE)
        for step in range(2):
            force = forces(pos, pos, str_cells, str_cells, global_cells)
            vel = vel + STEP * force
            pos = pos + STEP * vel
        return pos.reshape(3, ATOMS), vel.reshape(3, ATOMS)

    moved_pos, moved_vel = lax.map(walk, (positions, velocities))
    walkers = positions.shape[0]
    blocks = moved_pos.reshape(walkers, 3, N_SPACE, ATOMS_DEV)[:, :, :, :SITE_DEV]
    features = blocks.astype(jnp.bfloat16).astype(jnp.float32).reshape(walkers, -1)

    def one_row(feature):
        diff = feature[None, :] - features
        return jnp.sum(diff * diff, axis=1)

    distances = lax.map(one_row, features) / (3.0 * SITES)
    source_row = home[plan]
    counts = jnp.sum((plan[:, None] == plan[None, :]).astype(jnp.int32), axis=1)
    new_positions = moved_pos[source_row]
    new_velocities = moved_vel[source_row]
    new_weights = weights[source_row] / counts.astype(jnp.float32)
    return distances, new_positions, new_velocities, new_weights
```

```python
import functools

import jax
import jax.numpy as jnp
from jax import lax
from jax.experimental import pallas as pl
from jax.experimental.pallas import tpu as pltpu
from jax.sharding import PartitionSpec as P

HALO = 2
REACH = 2 * HALO + 1
SITES = 8192
STEP = 0.1
TILE = 128
ROWS = 40
MESH = pl.DeviceIdType.MESH


def kernel(
    n,
    nx,
    sites,
    pos,
    vel,
    stg,
    til,
    planv,
    wgt,
    plan,
    home,
    dist,
    npos,
    nvel,
    nwt,
    cast_a,
    cast_b,
    cast_s,
    mult,
    x1,
    v1,
    low_p,
    high_p,
    low_s,
    high_s,
    low_n,
    high_n,
    stage_x,
    stage_v,
    feat,
    feat_in,
    group,
    wide,
    own_rows,
    part,
    part_in,
    line,
    held_x,
    held_v,
    pick_x,
    pick_v,
    take_x,
    take_v,
    give_x,
    give_v,
    got_x,
    got_v,
    halo_send,
    halo_recv,
    f1_send,
    f1_recv,
    f2_send,
    f2_recv,
    f4_send,
    f4_recv,
    f5_send,
    f5_recv,
    s0_send,
    s0_recv,
    s1_send,
    s1_recv,
    s2_send,
    s2_recv,
    s3_send,
    s3_recv,
):
    cells = pos.shape[1]
    half = cells // 2
    members = 2 * n
    me = lax.axis_index("walker")
    here = lax.axis_index("space")
    core = me % 2
    yy = (me // 2) % n
    zz = me // members
    mine = me % members

    first = zz + core * (yy - zz)
    second = yy + core * (zz - yy)
    first_stride = 2 * (n - (n - 1) * core)
    second_stride = 2 * (1 + (n - 1) * core)
    pair = 1 - core
    twin = me + pair - core

    def member(m):
        return (zz * members + m, here)

    def level(z):
        return (z * members + mine, here)

    def along_first(p):
        return (p * first_stride + second * second_stride + core, here)

    def along_second(q):
        return (first * first_stride + q * second_stride + core, here)

    right = (me, (here + 1) % nx)
    left = (me, (here + nx - 1) % nx)

    barrier = pltpu.get_barrier_semaphore()

    def hello_member(k, _):
        pl.semaphore_signal(
            barrier, inc=1, device_id=member((mine + k) % members), device_id_type=MESH
        )
        return 0

    def hello_level(k, _):
        pl.semaphore_signal(
            barrier, inc=1, device_id=level((zz + k) % n), device_id_type=MESH
        )
        return 0

    def hello_space(k, _):
        pl.semaphore_signal(
            barrier, inc=1, device_id=(me, (here + k) % nx), device_id_type=MESH
        )
        return 0

    lax.fori_loop(1, nx, hello_space, 0)
    lax.fori_loop(1, members, hello_member, 0)
    lax.fori_loop(1, n, hello_level, 0)

    def remote(src, dst, send, recv, where):
        return pltpu.make_async_remote_copy(
            src_ref=src,
            dst_ref=dst,
            send_sem=send,
            recv_sem=recv,
            device_id=where,
            device_id_type=MESH,
        )

    rows = lax.broadcasted_iota(jnp.int32, til.shape, 0)
    shift = til[...] - rows
    for o in range(REACH):
        hits = jnp.sum((shift == o).astype(jnp.float32), axis=1, keepdims=True)
        mult[o] = jnp.broadcast_to(hits, (cells, TILE))

    def spread(dst, block, d, start):
        turned = block.T
        for g in range(block.shape[0]):
            value = jnp.broadcast_to(turned[:, g : g + 1], (TILE, TILE))
            if d is None:
                dst[start + g] = value
            else:
                dst[d, start + g] = value

    for d in range(3):
        spread(cast_a, pos[d], d, HALO)
    spread(cast_s, stg[...], None, HALO)

    def force(cast, source, g):
        at = [source[d, pl.ds(g, 1), :] for d in range(3)]
        total = [jnp.zeros((8, TILE), jnp.float32) for _ in range(3)]
        for o in range(REACH):
            acc = None
            for b in range(TILE // 32):
                piece = pl.ds(32 * b, 32)
                delta = [at[d] - cast[d, g + o, piece, :] for d in range(3)]
                q = delta[0] * delta[0] + 1.0
                q = q + delta[1] * delta[1]
                q = q + delta[2] * delta[2]
                w = pltpu.reciprocal(q * q, approx=True) * cast_s[g + o, piece, :]
                terms = [w * delta[d] for d in range(3)]
                if acc is None:
                    acc = terms
                else:
                    acc = [acc[d] + terms[d] for d in range(3)]
            count = mult[o, pl.ds(g, 1), :]
            for d in range(3):
                folded = acc[d][0:8] + acc[d][8:16] + (acc[d][16:24] + acc[d][24:32])
                total[d] = total[d] + count * folded
        weight = stg[pl.ds(g, 1), :]
        return [
            weight * jnp.sum(total[d], axis=0, keepdims=True) for d in range(3)
        ]

    def first_step(g):
        f = force(cast_a, pos, g)
        h = g // half
        for d in range(3):
            v = vel[d, pl.ds(g, 1), :] + STEP * f[d]
            x = pos[d, pl.ds(g, 1), :] + STEP * v
            v1[d, pl.ds(g, 1), :] = v
            x1[d, pl.ds(g, 1), :] = x
            stage_x[h, pl.ds(d * half + g - h * half, 1), :] = x

    def second_step(g, site):
        f = force(cast_b, x1, g)
        h = g // half
        for d in range(3):
            v = v1[d, pl.ds(g, 1), :] + STEP * f[d]
            x = x1[d, pl.ds(g, 1), :] + STEP * v
            stage_v[h, pl.ds(d * half + g - h * half, 1), :] = v
            if site:
                feat[g, pl.ds(d, 1), :] = x
        if site:

            @pl.when(g != mine)
            def _():
                remote(
                    feat.at[g],
                    feat_in.at[mine],
                    f1_send.at[g],
                    f1_recv.at[mine],
                    member(g),
                ).start()

    def run(step, low, high, turn=lambda k: k):
        def body(k, _):
            step(turn(k))
            return 0

        lax.fori_loop(low, high, body, 0)

    for h in range(2):
        stage_x[h, pl.ds(3 * half, ROWS - 3 * half), :] = jnp.broadcast_to(
            wgt[0], (ROWS - 3 * half, TILE)
        )
        stage_v[h, pl.ds(3 * half, ROWS - 3 * half), :] = jnp.zeros(
            (ROWS - 3 * half, TILE), jnp.float32
        )
    feat[...] = jnp.zeros(feat.shape, jnp.float32)

    run(first_step, HALO, 6)

    pl.semaphore_wait(barrier, (nx - 1) + (members - 1) + (n - 1))

    top = cells - 8
    halos = [
        remote(pos.at[:, pl.ds(top, 8), :], low_p, halo_send.at[0], halo_recv.at[0], right),
        remote(pos.at[:, pl.ds(0, 8), :], high_p, halo_send.at[1], halo_recv.at[1], left),
        remote(stg.at[pl.ds(top, 8), :], low_s, halo_send.at[2], halo_recv.at[2], right),
        remote(stg.at[pl.ds(0, 8), :], high_s, halo_send.at[3], halo_recv.at[3], left),
    ]
    for copy in halos:
        copy.start()

    run(first_step, 6, cells - HALO)

    for copy in halos:
        copy.wait()
    for d in range(3):
        spread(cast_a, low_p[d, 8 - HALO : 8, :], d, 0)
        spread(cast_a, high_p[d, 0:HALO, :], d, HALO + cells)
    spread(cast_s, low_s[8 - HALO : 8, :], None, 0)
    spread(cast_s, high_s[0:HALO, :], None, HALO + cells)

    run(first_step, 0, 2 * HALO, lambda k: k + (k // HALO) * (cells - 2 * HALO))

    nexts = [
        remote(x1.at[:, pl.ds(top, 8), :], low_n, halo_send.at[4], halo_recv.at[4], right),
        remote(x1.at[:, pl.ds(0, 8), :], high_n, halo_send.at[5], halo_recv.at[5], left),
    ]
    for copy in nexts:
        copy.start()

    slot_of_twin = 2 * second + core
    slot_of_pair = 2 * first + pair

    def to_twin(a, stage, held):
        return remote(
            stage.at[pair],
            held.at[slot_of_twin],
            s0_send.at[a],
            s0_recv.at[a],
            (twin, here),
        )

    def from_twin(a, stage, held):
        return remote(
            stage.at[pair],
            held.at[slot_of_pair],
            s0_send.at[a],
            s0_recv.at[a],
            (twin, here),
        )

    def out_first(a, held, p):
        return remote(
            held.at[pl.ds(2 * first, 2)],
            held.at[pl.ds(2 * first, 2)],
            s1_send.at[a * n + p],
            s1_recv.at[a * n + first],
            along_first(p),
        )

    def in_first(a, held, p):
        return remote(
            held.at[pl.ds(2 * p, 2)],
            held.at[pl.ds(2 * p, 2)],
            s1_send.at[a * n + p],
            s1_recv.at[a * n + p],
            along_first(p),
        )

    def out_second(a, pick, take, q):
        return remote(
            pick.at[q],
            take.at[second],
            s2_send.at[a * n + q],
            s2_recv.at[a * n + second],
            along_second(q),
        )

    def in_second(a, pick, take, q):
        return remote(
            pick.at[q],
            take.at[q],
            s2_send.at[a * n + q],
            s2_recv.at[a * n + q],
            along_second(q),
        )

    def others(count, own, act):
        def body(k, _):
            act((own + k) % count)
            return 0

        lax.fori_loop(1, count, body, 0)

    def source_parts(slot):
        row = home[plan[slot]]
        z = row // members
        y = (row // 2) % n
        c = row % 2
        return z + core * (y - z), y + core * (z - y), c

    def begin(a, stage, held):
        to_twin(a, stage, held).start()
        held[2 * first + core] = stage[core]

    def gather(a, stage, held):
        from_twin(a, stage, held).wait_recv()
        others(n, first, lambda p: out_first(a, held, p).start())

    def scatter(a, held, pick, take):
        others(n, first, lambda p: in_first(a, held, p).wait_recv())

        def choose(q, _):
            for c in range(2):
                slot = first * first_stride + q * second_stride + c
                p_src, _, c_src = source_parts(slot)
                pick[q, c] = held[2 * p_src + c_src]
            return 0

        lax.fori_loop(0, n, choose, 0)
        others(n, second, lambda q: out_second(a, pick, take, q).start())
        take[second] = pick[second]

    def finish(a, pick, take, give, got):
        others(n, second, lambda q: in_second(a, pick, take, q).wait_recv())
        _, q_twin, _ = source_parts(twin)
        give[...] = take[q_twin, pair]
        copy = remote(give, got, s3_send.at[a], s3_recv.at[a], (twin, here))
        copy.start()

    for d in range(3):
        spread(cast_b, x1[d], d, HALO)
    begin(0, stage_x, held_x)

    early = members - 2 * HALO
    run(lambda g: second_step(g, True), HALO, early)
    gather(0, stage_x, held_x)
    run(lambda g: second_step(g, True), early, members)

    for copy in nexts:
        copy.wait()
    for d in range(3):
        spread(cast_b, low_n[d, 8 - HALO : 8, :], d, 0)
        spread(cast_b, high_n[d, 0:HALO, :], d, HALO + cells)
    run(lambda g: second_step(g, True), 0, HALO)
    run(lambda g: second_step(g, False), members, cells - 2 * HALO)

    def f1(m):
        return remote(
            feat.at[m], feat_in.at[m], f1_send.at[m], f1_recv.at[m], member(m)
        )

    def f2(z):
        return remote(group.at[zz], group.at[zz], f2_send.at[z], f2_recv.at[zz], level(z))

    def f2_in(z):
        return remote(group.at[z], group.at[z], f2_send.at[z], f2_recv.at[z], level(z))

    feat_in[mine] = feat[mine]
    others(members, mine, lambda m: f1(m).wait_recv())
    for d in range(3):
        group[zz, :, TILE * d : TILE * (d + 1)] = feat_in[:, d, :].astype(jnp.bfloat16)
    others(n, zz, lambda z: f2(z).start())

    scatter(0, held_x, pick_x, take_x)
    run(lambda g: second_step(g, False), cells - 2 * HALO, cells)
    begin(1, stage_v, held_v)
    gather(1, stage_v, held_v)

    others(n, zz, lambda z: f2_in(z).wait_recv())
    walkers = n * members
    wide[...] = group[...].astype(jnp.float32).reshape(walkers, 3 * TILE)
    for d in range(3):
        own_rows[d] = group[zz, :, TILE * d : TILE * (d + 1)].astype(jnp.float32)
    lanes = lax.broadcasted_iota(jnp.int32, (walkers, TILE), 1)

    def row_of(r, acc):
        total = None
        for d in range(3):
            part_of = pl.ds(TILE * d, TILE)
            diff = wide[:, part_of] - own_rows[d, pl.ds(r, 1), :]
            square = diff * diff
            total = square if total is None else total + square
        return jnp.where(lanes == r, jnp.sum(total, axis=1, keepdims=True), acc)

    sums = lax.fori_loop(0, members, row_of, jnp.zeros((walkers, TILE), jnp.float32)).T
    for r in range(members):
        part[r, :, 0:walkers] = jnp.broadcast_to(sums[r : r + 1], (8, walkers))

    def f4(m):
        return remote(
            part.at[m], part_in.at[mine], f4_send.at[m], f4_recv.at[mine], member(m)
        )

    def f4_in(m):
        return remote(part.at[m], part_in.at[m], f4_send.at[m], f4_recv.at[m], member(m))

    others(members, mine, lambda m: f4(m).start())
    part_in[mine] = part[mine]

    finish(0, pick_x, take_x, give_x, got_x)
    others(members, mine, lambda m: f4_in(m).wait_recv())
    row = part_in[0]
    for m in range(1, members):
        row = row + part_in[m]
    line[here] = row

    def f5(s):
        return remote(
            line.at[here], line.at[here], f5_send.at[s], f5_recv.at[here], (me, s)
        )

    def f5_in(s):
        return remote(line.at[s], line.at[s], f5_send.at[s], f5_recv.at[s], (me, s))

    others(nx, here, lambda s: f5(s).start())

    scatter(1, held_v, pick_v, take_v)

    others(nx, here, lambda s: f5_in(s).wait_recv())
    row = line[0, 0:1, 0:walkers]
    for s in range(1, nx):
        row = row + line[s, 0:1, 0:walkers]
    row = row / (3.0 * sites)
    share = walkers // nx
    mine_of = row[:, 0:share]
    for s in range(1, nx):
        mine_of = jnp.where(here == s, row[:, share * s : share * (s + 1)], mine_of)
    dist[...] = mine_of

    finish(1, pick_v, take_v, give_v, got_v)

    _, q_own, _ = source_parts(me)
    own_x = take_x[q_own, core]
    own_v = take_v[q_own, core]
    same = (planv[...] == plan[me]).astype(jnp.float32)
    nwt[...] = own_x[3 * half : 3 * half + 1, 0:1] / jnp.sum(same, axis=1, keepdims=True)

    def other_half(a, give, got):
        return remote(give, got, s3_send.at[a], s3_recv.at[a], (twin, here))

    other_half(0, give_x, got_x).wait_recv()
    other_half(1, give_v, got_v).wait_recv()
    far_x = got_x[...]
    far_v = got_v[...]
    for h in range(2):
        v = jnp.where(core == h, own_v, far_v)
        x = jnp.where(core == h, own_x, far_x) + STEP * v
        for d in range(3):
            nvel[d, half * h : half * (h + 1), :] = v[half * d : half * (d + 1)]
            npos[d, half * h : half * (h + 1), :] = x[half * d : half * (d + 1)]

    for a, stage, held, pick, take, give, got in (
        (0, stage_x, held_x, pick_x, take_x, give_x, got_x),
        (1, stage_v, held_v, pick_v, take_v, give_v, got_v),
    ):
        to_twin(a, stage, held).wait_send()
        others(n, first, lambda p: out_first(a, held, p).wait_send())
        others(n, second, lambda q: out_second(a, pick, take, q).wait_send())
        other_half(a, give, got).wait_send()
    others(members, mine, lambda m: f1(m).wait_send())
    others(n, zz, lambda z: f2(z).wait_send())
    others(members, mine, lambda m: f4(m).wait_send())
    others(nx, here, lambda s: f5(s).wait_send())


def solution(mesh):
    walkers = mesh.shape["walker"]
    nx = mesh.shape["space"]
    n = 1
    while 2 * n * n < walkers:
        n += 1
    members = 2 * n

    def shards(positions, velocities, weights, strength, tiles, plan, home):
        cells = tiles.shape[0]
        ext = cells + 2 * HALO
        f32 = jnp.float32
        vmem = pl.BlockSpec(memory_space=pltpu.VMEM)
        smem = pl.BlockSpec(memory_space=pltpu.SMEM)
        dma = pltpu.SemaphoreType.DMA
        sites = members * TILE * nx
        block = jax.ShapeDtypeStruct((3, cells, TILE), f32)
        dist, npos, nvel, nwt = pl.pallas_call(
            functools.partial(kernel, n, nx, sites),
            out_shape=(
                jax.ShapeDtypeStruct((1, walkers // nx), f32),
                block,
                block,
                jax.ShapeDtypeStruct((1, 1), f32),
            ),
            in_specs=[vmem] * 5 + [smem] * 3,
            out_specs=(vmem,) * 4,
            scratch_shapes=[
                pltpu.VMEM((3, ext, TILE, TILE), f32),
                pltpu.VMEM((3, ext, TILE, TILE), f32),
                pltpu.VMEM((ext, TILE, TILE), f32),
                pltpu.VMEM((REACH, cells, TILE), f32),
                pltpu.VMEM((3, cells, TILE), f32),
                pltpu.VMEM((3, cells, TILE), f32),
                pltpu.VMEM((3, 8, TILE), f32),
                pltpu.VMEM((3, 8, TILE), f32),
                pltpu.VMEM((8, TILE), f32),
                pltpu.VMEM((8, TILE), f32),
                pltpu.VMEM((3, 8, TILE), f32),
                pltpu.VMEM((3, 8, TILE), f32),
                pltpu.VMEM((2, ROWS, TILE), f32),
                pltpu.VMEM((2, ROWS, TILE), f32),
                pltpu.VMEM((members, 8, TILE), f32),
                pltpu.VMEM((members, 8, TILE), f32),
                pltpu.VMEM((n, members, 3 * TILE), jnp.bfloat16),
                pltpu.VMEM((walkers, 3 * TILE), f32),
                pltpu.VMEM((3, members, TILE), f32),
                pltpu.VMEM((members, 8, TILE), f32),
                pltpu.VMEM((members, 8, TILE), f32),
                pltpu.VMEM((nx, 8, TILE), f32),
                pltpu.VMEM((members, ROWS, TILE), f32),
                pltpu.VMEM((members, ROWS, TILE), f32),
                pltpu.VMEM((n, 2, ROWS, TILE), f32),
                pltpu.VMEM((n, 2, ROWS, TILE), f32),
                pltpu.VMEM((n, 2, ROWS, TILE), f32),
                pltpu.VMEM((n, 2, ROWS, TILE), f32),
                pltpu.VMEM((ROWS, TILE), f32),
                pltpu.VMEM((ROWS, TILE), f32),
                pltpu.VMEM((ROWS, TILE), f32),
                pltpu.VMEM((ROWS, TILE), f32),
                dma((6,)),
                dma((6,)),
                dma((members,)),
                dma((members,)),
                dma((n,)),
                dma((n,)),
                dma((members,)),
                dma((members,)),
                dma((nx,)),
                dma((nx,)),
                dma((2,)),
                dma((2,)),
                dma((2 * n,)),
                dma((2 * n,)),
                dma((2 * n,)),
                dma((2 * n,)),
                dma((2,)),
                dma((2,)),
            ],
            compiler_params=pltpu.CompilerParams(
                collective_id=0,
                has_side_effects=True,
                vmem_limit_bytes=40 * 1024 * 1024,
            ),
        )(
            positions.reshape(3, cells, TILE),
            velocities.reshape(3, cells, TILE),
            strength.reshape(cells, TILE),
            tiles,
            plan.reshape(1, walkers),
            weights,
            plan,
            home,
        )
        return (
            dist,
            npos.reshape(1, 3, cells * TILE),
            nvel.reshape(1, 3, cells * TILE),
            nwt.reshape(1),
        )

    return jax.shard_map(
        shards,
        mesh=mesh,
        in_specs=(
            P("walker", None, "space"),
            P("walker", None, "space"),
            P("walker"),
            P("space"),
            P("space", None),
            P(),
            P(),
        ),
        out_specs=(
            P("walker", "space"),
            P("walker", None, "space"),
            P("walker", None, "space"),
            P("walker"),
        ),
        check_vma=False,
    )
```

```python
import functools

import jax
import jax.numpy as jnp
from jax import lax
from jax.experimental import pallas as pl
from jax.experimental.pallas import tpu as pltpu
from jax.sharding import PartitionSpec as P

HALO = 2
REACH = 2 * HALO + 1
STEP = 0.1
TILE = 128
ROWS = 40
SPLIT = 24
KEYS = 48
CHUNK = 64
MESH = pl.DeviceIdType.MESH


def kernel(
    n,
    nx,
    pos_in,
    vel_in,
    stg_in,
    til_in,
    row_in,
    plan_in,
    home_in,
    wgt,
    dist,
    npos,
    nvel,
    nwt,
    pos,
    vel,
    stg,
    til,
    planv,
    plan,
    home,
    side_j,
    next_j,
    side_i,
    next_i,
    base_w,
    next_w,
    mult,
    x1,
    v1,
    low_p,
    high_p,
    low_s,
    high_s,
    low_n,
    high_n,
    stage_x,
    stage_va,
    stage_vb,
    feat,
    feat_in,
    group,
    wide,
    own_rows,
    part,
    part_in,
    line,
    held_x,
    held_va,
    held_vb,
    pick_x,
    pick_va,
    pick_vb,
    take_x,
    take_va,
    take_vb,
    load_sem,
    halo_send,
    halo_recv,
    feat_send,
    feat_recv,
    one_send,
    one_recv,
    two_send,
    two_recv,
):
    cells = pos.shape[1]
    members = 2 * n
    walkers = members * n
    near = cells - 8
    sites = members * TILE * nx
    me = lax.axis_index("walker")
    here = lax.axis_index("space")
    core = me % 2
    yy = (me // 2) % n
    zz = me // members
    mine = me % members

    first = zz + core * (yy - zz)
    second = yy + core * (zz - yy)
    first_stride = 2 * (n - (n - 1) * core)
    second_stride = 2 * (1 + (n - 1) * core)
    pair = 1 - core
    twin = me + pair - core

    loads = [
        pltpu.make_async_copy(src, dst, load_sem.at[i])
        for i, (src, dst) in enumerate(
            ((pos_in, pos), (stg_in, stg), (til_in, til), (vel_in, vel), (row_in, planv), (plan_in, plan), (home_in, home))
        )
    ]
    for copy in loads:
        copy.start()

    def member(m):
        return (zz * members + m, here)

    def level(z):
        return (z * members + mine, here)

    right = (me, (here + 1) % nx)
    left = (me, (here + nx - 1) % nx)

    def others(count, own, act):
        def body(k, _):
            act((own + k) % count)
            return 0

        lax.fori_loop(1, count, body, 0)

    barrier = pltpu.get_barrier_semaphore()

    def hello(where):
        pl.semaphore_signal(barrier, inc=1, device_id=where, device_id_type=MESH)

    others(nx, here, lambda s: hello((me, s)))
    others(members, mine, lambda m: hello(member(m)))

    def hello_level(z):
        hello(level(z))
        hello((z * members + mine + pair - core, here))

    others(n, zz, hello_level)

    def remote(src, dst, send, recv, where):
        return pltpu.make_async_remote_copy(
            src_ref=src,
            dst_ref=dst,
            send_sem=send,
            recv_sem=recv,
            device_id=where,
            device_id_type=MESH,
        )

    def wait_all(ref, sem):
        pltpu.make_async_copy(ref, ref, sem).wait()

    for h in range(2):
        stage_x[h, pl.ds(36, 4), :] = jnp.broadcast_to(wgt[0], (4, TILE))
        stage_vb[h, pl.ds(12, 4), :] = jnp.zeros((4, TILE), jnp.float32)
    feat[...] = jnp.zeros(feat.shape, jnp.float32)
    x1[...] = jnp.zeros(x1.shape, jnp.float32)

    for copy in loads[:3]:
        copy.wait()

    shift = til[...] - lax.broadcasted_iota(jnp.int32, til.shape, 0)
    hits = [
        jnp.broadcast_to(
            jnp.sum((shift == o).astype(jnp.float32), axis=1, keepdims=True), (cells, TILE)
        )
        for o in range(REACH)
    ]
    none = jnp.zeros((4, TILE), jnp.float32)
    for k in range(REACH + 1):
        for p in range(cells // 2):
            for row, g, o in ((0, 2 * p, k), (4, 2 * p + 1, k - 1)):
                value = none
                if 0 <= o < REACH:
                    value = jnp.broadcast_to(hits[o][g : g + 1], (4, TILE))
                mult[k, p, row : row + 4, :] = value

    def thirds(x):
        high = x.astype(jnp.bfloat16).astype(jnp.float32)
        rest = x - high
        middle = rest.astype(jnp.bfloat16).astype(jnp.float32)
        return high, middle, rest - middle

    one_row = jnp.ones((1, TILE), jnp.float32)
    three_rows = jnp.zeros((3, TILE), jnp.float32)

    def prepare(to_j, to_w, cell, x, s, to_i=None):
        norm = x[0] * x[0] + x[1] * x[1] + x[2] * x[2]
        a, b, c = thirds(
            jnp.concatenate([x[0], x[1], x[2], norm + 1.0, one_row, three_rows], axis=0)
        )
        keys = jnp.concatenate([a, a, b, b, a, c], axis=0).T
        to_j[pl.ds(pl.multiple_of(cell * TILE, TILE), TILE), :] = keys.astype(jnp.bfloat16)
        four = [s, s * x[0], s * x[1], s * x[2]]
        to_w[cell] = jnp.concatenate(four + four, axis=0)
        if to_i is not None:
            a, b, c = thirds(
                jnp.concatenate(
                    [-2.0 * x[0], -2.0 * x[1], -2.0 * x[2], one_row, norm, three_rows], axis=0
                )
            )
            ref, p, lane = to_i
            ref[p, :, TILE * lane : TILE * (lane + 1)] = jnp.concatenate(
                [a, b, a, b, c, a], axis=0
            ).astype(jnp.bfloat16)

    def prepare_pair(source, to_j, to_w, to_i, p):
        for lane in range(2):
            g = 2 * p + lane
            prepare(
                to_j,
                to_w,
                g + HALO,
                [source[d, pl.ds(g, 1), :] for d in range(3)],
                stg[pl.ds(g, 1), :],
                (to_i, p, lane),
            )

    def prepare_own(p, _):
        prepare_pair(pos, side_j, base_w, side_i, p)
        return 0

    lax.fori_loop(0, cells // 2, prepare_own, 0)
    for copy in loads[3:]:
        copy.wait()

    def prepare_halo(to_j, to_w, low, high):
        for k in range(HALO):
            for base, at, pos_of, str_of in (
                (0, 8 - HALO, low, low_s),
                (HALO + cells, 0, high, high_s),
            ):
                prepare(
                    to_j,
                    to_w,
                    base + k,
                    [pos_of[d, at + k : at + k + 1, :] for d in range(3)],
                    str_of[at + k : at + k + 1, :],
                )

    def force(of_j, of_i, of_w, source, p):
        weights = []
        for k in range(REACH + 1):
            parts = thirds(mult[k, p] * of_w[2 * p + k])
            weights.append(
                jnp.concatenate(list(parts) + [jnp.zeros((8, TILE), jnp.float32)], axis=0)
            )
        weights = jnp.concatenate(weights, axis=1).astype(jnp.bfloat16)
        keys_i = of_i[p]
        total = None
        for k in range((REACH + 1) // 2):
            highs, lows = [], []
            for b in range(2 * TILE // CHUNK):
                at = pl.multiple_of(p * 2 * TILE, 2 * TILE) + k * 2 * TILE + b * CHUNK
                q = jnp.dot(
                    of_j[pl.ds(at, CHUNK), :], keys_i, preferred_element_type=jnp.float32
                )
                f = pltpu.reciprocal(q * q, approx=True)
                high = f.astype(jnp.bfloat16)
                highs.append(high)
                lows.append((f - high.astype(jnp.float32)).astype(jnp.bfloat16))
            w = weights[:, 2 * TILE * k : 2 * TILE * (k + 1)]
            for piece in (highs, lows):
                term = jnp.dot(
                    w, jnp.concatenate(piece, axis=0), preferred_element_type=jnp.float32
                )
                total = term if total is None else total + term
        total = total[0:8] + (total[8:16] + total[16:24])
        result = []
        for lane in range(2):
            g = 2 * p + lane
            part_of = total[4 * lane : 4 * lane + 4, TILE * lane : TILE * (lane + 1)]
            s = stg[pl.ds(g, 1), :]
            result.append(
                [
                    s * (source[d, pl.ds(g, 1), :] * part_of[0:1] - part_of[d + 1 : d + 2])
                    for d in range(3)
                ]
            )
        return result

    def stage_at(g):
        inner = g < near
        h = jnp.where(inner, g // 8, (g - near) // 4)
        base = jnp.where(inner, g % 8, SPLIT + (g - near) % 4)
        return h, base, jnp.where(inner, 8, 4)

    top = cells - 8
    halos = [
        remote(pos.at[:, pl.ds(top, 8), :], low_p, halo_send.at[0], halo_recv.at[0], right),
        remote(pos.at[:, pl.ds(0, 8), :], high_p, halo_send.at[1], halo_recv.at[1], left),
        remote(stg.at[pl.ds(top, 8), :], low_s, halo_send.at[2], halo_recv.at[2], right),
        remote(stg.at[pl.ds(0, 8), :], high_s, halo_send.at[3], halo_recv.at[3], left),
    ]
    nexts = [
        remote(x1.at[:, pl.ds(top, 8), :], low_n, halo_send.at[4], halo_recv.at[4], right),
        remote(x1.at[:, pl.ds(0, 8), :], high_n, halo_send.at[5], halo_recv.at[5], left),
    ]

    pairs = cells // 2

    def order_one(t):
        return (t + 1) % pairs

    def first_step(t, _):
        @pl.when(t == 2)
        def _():
            pl.semaphore_wait(barrier, (nx - 1) + (members - 1) + 2 * (n - 1))
            for copy in halos:
                copy.start()

        @pl.when(t == pairs - 2)
        def _():
            for copy in halos:
                copy.wait()
            prepare_halo(side_j, base_w, low_p, high_p)

        p = order_one(t)
        prepare_pair(x1, next_j, next_w, next_i, order_one(t + pairs - 1))
        f = force(side_j, side_i, base_w, pos, p)
        for lane in range(2):
            g = 2 * p + lane
            h, base, stride = stage_at(g)
            for d in range(3):
                v = vel[d, pl.ds(g, 1), :] + STEP * f[lane][d]
                x = pos[d, pl.ds(g, 1), :] + STEP * v
                v1[d, pl.ds(g, 1), :] = v
                x1[d, pl.ds(g, 1), :] = x
                stage_x[h, pl.ds(base + d * stride, 1), :] = x
        return 0

    lax.fori_loop(0, pairs, first_step, 0)
    for copy in nexts:
        copy.start()

    def spread_state(a, stage, held):
        for h, own, low, step in ((0, zz, 2 * yy, members), (1, yy, zz * members + 1, 2)):

            def send(p, h=h, own=own, low=low, step=step):
                remote(
                    stage.at[h],
                    held.at[2 * own + core],
                    one_send.at[a],
                    one_recv.at[a],
                    (low + p * step, here),
                ).start()

            others(n, own, send)
        remote(
            stage.at[pair],
            held.at[2 * second + core],
            one_send.at[a],
            one_recv.at[a],
            (twin, here),
        ).start()
        held[2 * first + core] = stage[core]

    def source_of(slot):
        row = home[plan[slot]]
        return row // members, (row // 2) % n, row % 2

    def hand_on(a, held, pick, take):
        wait_all(held.at[pl.ds(0, members - 1)], one_recv.at[a])

        def choose(q, _):
            for c in range(2):
                slot = first * first_stride + q * second_stride + c
                z, y, c_src = source_of(slot)
                p = z + core * (y - z)
                pick[2 * q + c] = held[2 * p + c_src]

                @pl.when(slot != me)
                def _(slot=slot, c=c):
                    remote(
                        pick.at[2 * q + c],
                        take.at[core * n + second],
                        two_send.at[a],
                        two_recv.at[a],
                        (slot, here),
                    ).start()

            return 0

        lax.fori_loop(0, n, choose, 0)
        take[core * n + second] = pick[2 * second + core]

    spread_state(0, stage_x, held_x)
    prepare_pair(x1, next_j, next_w, next_i, order_one(pairs - 1))

    def share_features():
        feat_in[mine] = feat[mine]
        wait_all(feat_in.at[pl.ds(0, members - 1)], feat_recv.at[0])
        for d in range(3):
            group[zz, :, TILE * d : TILE * (d + 1)] = feat_in[:, d, :].astype(jnp.bfloat16)
        others(
            n,
            zz,
            lambda z: remote(
                group.at[zz], group.at[zz], feat_send.at[1], feat_recv.at[1], level(z)
            ).start(),
        )

    near_pairs = near // 2

    def second_step(t, _):
        @pl.when(t == near_pairs - 1)
        def _():
            for copy in nexts:
                copy.wait()
            prepare_halo(next_j, next_w, low_n, high_n)

        @pl.when(t == near_pairs)
        def _():
            spread_state(1, stage_va, held_va)

        @pl.when(t == near_pairs + 1)
        def _():
            share_features()
            hand_on(0, held_x, pick_x, take_x)

        p = jnp.where(t < near_pairs, (t + 1) % near_pairs, t)
        f = force(next_j, next_i, next_w, x1, p)
        for lane in range(2):
            g = 2 * p + lane
            h, base, stride = stage_at(g)
            for d in range(3):
                v = v1[d, pl.ds(g, 1), :] + STEP * f[lane][d]
                x = x1[d, pl.ds(g, 1), :] + STEP * v

                @pl.when(t < near_pairs)
                def _(v=v, h=h, base=base, d=d):
                    stage_va[h, pl.ds(base + 8 * d, 1), :] = v

                @pl.when(t >= near_pairs)
                def _(v=v, h=h, base=base, d=d):
                    stage_vb[h, pl.ds(base - SPLIT + 4 * d, 1), :] = v

                feat[g, pl.ds(d, 1), :] = x

            @pl.when((g < members) & (g != mine))
            def _(g=g):
                remote(
                    feat.at[g], feat_in.at[mine], feat_send.at[0], feat_recv.at[0], member(g)
                ).start()

        return 0

    lax.fori_loop(0, pairs, second_step, 0)
    spread_state(2, stage_vb, held_vb)
    hand_on(1, held_va, pick_va, take_va)

    wait_all(group.at[pl.ds(0, n - 1)], feat_recv.at[1])
    wide[...] = group[...].astype(jnp.float32).reshape(walkers, 3 * TILE)
    for d in range(3):
        own_rows[d] = group[zz, :, TILE * d : TILE * (d + 1)].astype(jnp.float32)
    lanes = lax.broadcasted_iota(jnp.int32, (walkers, TILE), 1)

    def row_of(r, acc):
        total = None
        for d in range(3):
            diff = wide[:, TILE * d : TILE * (d + 1)] - own_rows[d, pl.ds(r, 1), :]
            square = diff * diff
            total = square if total is None else total + square
        return jnp.where(lanes == r, jnp.sum(total, axis=1, keepdims=True), acc)

    sums = lax.fori_loop(0, members, row_of, jnp.zeros((walkers, TILE), jnp.float32)).T
    for r in range(members):
        part[r, :, 0:walkers] = jnp.broadcast_to(sums[r : r + 1], (8, walkers))
    others(
        members,
        mine,
        lambda m: remote(
            part.at[m], part_in.at[mine], feat_send.at[2], feat_recv.at[2], member(m)
        ).start(),
    )
    part_in[mine] = part[mine]

    hand_on(2, held_vb, pick_vb, take_vb)

    wait_all(part_in.at[pl.ds(0, members - 1)], feat_recv.at[2])
    row = part_in[0]
    for m in range(1, members):
        row = row + part_in[m]
    line[here] = row
    others(
        nx,
        here,
        lambda s: remote(
            line.at[here], line.at[here], feat_send.at[3], feat_recv.at[3], (me, s)
        ).start(),
    )
    wait_all(line.at[pl.ds(0, nx - 1)], feat_recv.at[3])
    row = line[0, 0:1, 0:walkers]
    for s in range(1, nx):
        row = row + line[s, 0:1, 0:walkers]
    row = row / (3.0 * sites)
    share = walkers // nx
    mine_of = row[:, 0:share]
    for s in range(1, nx):
        mine_of = jnp.where(here == s, row[:, share * s : share * (s + 1)], mine_of)
    dist[...] = mine_of

    for a, take in enumerate((take_x, take_va, take_vb)):
        wait_all(take.at[pl.ds(0, members - 1)], two_recv.at[a])

    z, y, _ = source_of(me)
    for h, index in ((0, y), (1, n + z)):
        x = take_x[index]
        va = take_va[index]
        vb = take_vb[index]
        if h == 0:
            same = (planv[...] == plan[me]).astype(jnp.float32)
            nwt[...] = x[36:37, 0:1] / jnp.sum(same, axis=1, keepdims=True)
        xa = x[0:SPLIT] + STEP * va
        xb = x[SPLIT:ROWS] + STEP * vb
        for out, of_a, of_b in ((nvel, va, vb), (npos, xa, xb)):
            for d in range(3):
                out[d, 8 * h : 8 * h + 8, :] = of_a[8 * d : 8 * d + 8]
                out[d, near + 4 * h : near + 4 * h + 4, :] = of_b[4 * d : 4 * d + 4]

    for a, held in enumerate((held_x, held_va, held_vb)):
        wait_all(held.at[pl.ds(0, members - 1)], one_send.at[a])
        wait_all(held.at[pl.ds(0, members - 1)], two_send.at[a])
    wait_all(feat_in.at[pl.ds(0, members - 1)], feat_send.at[0])
    wait_all(group.at[pl.ds(0, n - 1)], feat_send.at[1])
    wait_all(part_in.at[pl.ds(0, members - 1)], feat_send.at[2])
    wait_all(line.at[pl.ds(0, nx - 1)], feat_send.at[3])


def solution(mesh):
    walkers = mesh.shape["walker"]
    nx = mesh.shape["space"]
    n = 1
    while 2 * n * n < walkers:
        n += 1
    members = 2 * n

    def shards(positions, velocities, weights, strength, tiles, plan, home):
        cells = tiles.shape[0]
        ext = cells + 2 * HALO
        f32 = jnp.float32
        vmem = pl.BlockSpec(memory_space=pltpu.VMEM)
        smem = pl.BlockSpec(memory_space=pltpu.SMEM)
        hbm = pl.BlockSpec(memory_space=pltpu.HBM)
        dma = pltpu.SemaphoreType.DMA
        block = jax.ShapeDtypeStruct((3, cells, TILE), f32)

        def pinned(x):
            return pltpu.with_memory_space_constraint(x, pltpu.HBM)

        def room(*shape, kind=f32):
            return pltpu.VMEM(shape, kind)

        dist, npos, nvel, nwt = pl.pallas_call(
            functools.partial(kernel, n, nx),
            out_shape=(
                jax.ShapeDtypeStruct((1, walkers // nx), f32),
                block,
                block,
                jax.ShapeDtypeStruct((1, 1), f32),
            ),
            in_specs=[hbm] * 7 + [smem],
            out_specs=(vmem,) * 4,
            scratch_shapes=[
                room(3, cells, TILE),
                room(3, cells, TILE),
                room(cells, TILE),
                room(*tiles.shape, kind=jnp.int32),
                room(1, walkers, kind=jnp.int32),
                pltpu.SMEM((walkers,), jnp.int32),
                pltpu.SMEM((walkers,), jnp.int32),
                room(ext * TILE, KEYS, kind=jnp.bfloat16),
                room(ext * TILE, KEYS, kind=jnp.bfloat16),
                room(cells // 2, KEYS, 2 * TILE, kind=jnp.bfloat16),
                room(cells // 2, KEYS, 2 * TILE, kind=jnp.bfloat16),
                room(ext, 8, TILE),
                room(ext, 8, TILE),
                room(REACH + 1, cells // 2, 8, TILE),
                room(3, cells, TILE),
                room(3, cells, TILE),
                room(3, 8, TILE),
                room(3, 8, TILE),
                room(8, TILE),
                room(8, TILE),
                room(3, 8, TILE),
                room(3, 8, TILE),
                room(2, ROWS, TILE),
                room(2, SPLIT, TILE),
                room(2, ROWS - SPLIT, TILE),
                room(cells, 8, TILE),
                room(members, 8, TILE),
                room(n, members, 3 * TILE, kind=jnp.bfloat16),
                room(walkers, 3 * TILE),
                room(3, members, TILE),
                room(members, 8, TILE),
                room(members, 8, TILE),
                room(nx, 8, TILE),
                room(members, ROWS, TILE),
                room(members, SPLIT, TILE),
                room(members, ROWS - SPLIT, TILE),
                room(members, ROWS, TILE),
                room(members, SPLIT, TILE),
                room(members, ROWS - SPLIT, TILE),
                room(members, ROWS, TILE),
                room(members, SPLIT, TILE),
                room(members, ROWS - SPLIT, TILE),
                dma((7,)),
                dma((6,)),
                dma((6,)),
                dma((4,)),
                dma((4,)),
                dma((3,)),
                dma((3,)),
                dma((3,)),
                dma((3,)),
            ],
            compiler_params=pltpu.CompilerParams(
                collective_id=0,
                has_side_effects=True,
                vmem_limit_bytes=40 * 1024 * 1024,
            ),
        )(
            pinned(positions.reshape(3, cells, TILE)),
            pinned(velocities.reshape(3, cells, TILE)),
            pinned(strength.reshape(cells, TILE)),
            pinned(tiles),
            pinned(plan.reshape(1, walkers)),
            pinned(plan),
            pinned(home),
            weights,
        )
        return (
            dist,
            npos.reshape(1, 3, cells * TILE),
            nvel.reshape(1, 3, cells * TILE),
            nwt.reshape(1),
        )

    return jax.shard_map(
        shards,
        mesh=mesh,
        in_specs=(
            P("walker", None, "space"),
            P("walker", None, "space"),
            P("walker"),
            P("space"),
            P("space", None),
            P(),
            P(),
        ),
        out_specs=(
            P("walker", "space"),
            P("walker", None, "space"),
            P("walker", None, "space"),
            P("walker"),
        ),
        check_vma=False,
    )
```

```python
import functools

import jax
import jax.numpy as jnp
from jax import lax
from jax.experimental import pallas as pl
from jax.experimental.pallas import tpu as pltpu
from jax.sharding import PartitionSpec as P

HALO = 2
REACH = 2 * HALO + 1
STEP = 0.1
TILE = 128
ROWS = 40
SPLIT = 24
KEYS = 48
CHUNK = 32
MESH = pl.DeviceIdType.MESH


def kernel(
    n,
    nx,
    pos_in,
    vel_in,
    stg_in,
    til_in,
    row_in,
    plan_in,
    home_in,
    wgt,
    dist,
    npos,
    nvel,
    nwt,
    pos,
    vel,
    stg,
    til,
    planv,
    plan,
    home,
    side_j,
    next_j,
    side_i,
    next_i,
    base_w,
    next_w,
    mult,
    x1,
    v1,
    low_p,
    high_p,
    low_s,
    high_s,
    low_n,
    high_n,
    stage_x,
    stage_va,
    stage_vb,
    feat,
    feat_in,
    group,
    wide,
    own_rows,
    part,
    part_in,
    line,
    held_x,
    held_va,
    held_vb,
    pick_x,
    pick_va,
    pick_vb,
    take_x,
    take_va,
    take_vb,
    load_sem,
    halo_send,
    halo_recv,
    feat_send,
    feat_recv,
    one_send,
    one_recv,
    two_send,
    two_recv,
):
    cells = pos.shape[1]
    members = 2 * n
    walkers = members * n
    near = cells - 8
    sites = members * TILE * nx
    me = lax.axis_index("walker")
    here = lax.axis_index("space")
    core = me % 2
    yy = (me // 2) % n
    zz = me // members
    mine = me % members

    first = zz + core * (yy - zz)
    second = yy + core * (zz - yy)
    first_stride = 2 * (n - (n - 1) * core)
    second_stride = 2 * (1 + (n - 1) * core)
    pair = 1 - core
    twin = me + pair - core

    loads = [
        pltpu.make_async_copy(src, dst, load_sem.at[i])
        for i, (src, dst) in enumerate(
            ((pos_in, pos), (stg_in, stg), (til_in, til), (vel_in, vel), (row_in, planv), (plan_in, plan), (home_in, home))
        )
    ]
    for copy in loads:
        copy.start()

    def member(m):
        return (zz * members + m, here)

    def level(z):
        return (z * members + mine, here)

    right = (me, (here + 1) % nx)
    left = (me, (here + nx - 1) % nx)

    def others(count, own, act):
        for k in range(1, count):
            act(lax.rem(own + k, count))

    barrier = pltpu.get_barrier_semaphore()

    def hello(where):
        pl.semaphore_signal(barrier, inc=1, device_id=where, device_id_type=MESH)

    others(nx, here, lambda s: hello((me, s)))
    others(members, mine, lambda m: hello(member(m)))

    def hello_level(z):
        hello(level(z))
        hello((z * members + mine + pair - core, here))

    others(n, zz, hello_level)

    def remote(src, dst, send, recv, where):
        return pltpu.make_async_remote_copy(
            src_ref=src,
            dst_ref=dst,
            send_sem=send,
            recv_sem=recv,
            device_id=where,
            device_id_type=MESH,
        )

    def wait_all(ref, sem):
        pltpu.make_async_copy(ref, ref, sem).wait()

    for h in range(2):
        stage_x[h, pl.ds(36, 4), :] = jnp.broadcast_to(wgt[0], (4, TILE))
        stage_vb[h, pl.ds(12, 4), :] = jnp.zeros((4, TILE), jnp.float32)
    feat[...] = jnp.zeros(feat.shape, jnp.float32)
    x1[...] = jnp.zeros(x1.shape, jnp.float32)

    for copy in loads[:3]:
        copy.wait()

    shift = til[...] - lax.broadcasted_iota(jnp.int32, til.shape, 0)
    hits = [
        jnp.broadcast_to(
            jnp.sum((shift == o).astype(jnp.float32), axis=1, keepdims=True), (cells, TILE)
        )
        for o in range(REACH)
    ]
    none = jnp.zeros((4, TILE), jnp.float32)
    for k in range(REACH + 1):
        for p in range(cells // 2):
            for row, g, o in ((0, 2 * p, k), (4, 2 * p + 1, k - 1)):
                value = none
                if 0 <= o < REACH:
                    value = jnp.broadcast_to(hits[o][g : g + 1], (4, TILE))
                mult[k, p, row : row + 4, :] = value

    def thirds(x):
        high = x.astype(jnp.bfloat16).astype(jnp.float32)
        rest = x - high
        middle = rest.astype(jnp.bfloat16).astype(jnp.float32)
        return high, middle, rest - middle

    one_row = jnp.ones((1, TILE), jnp.float32)
    three_rows = jnp.zeros((3, TILE), jnp.float32)

    def prepare(to_j, to_w, cell, x, s, to_i=None):
        norm = x[0] * x[0] + x[1] * x[1] + x[2] * x[2]
        a, b, c = thirds(
            jnp.concatenate([x[0], x[1], x[2], norm + 1.0, one_row, three_rows], axis=0)
        )
        keys = jnp.concatenate([a, a, b, b, a, c], axis=0).T
        to_j[pl.ds(pl.multiple_of(cell * TILE, TILE), TILE), :] = keys.astype(jnp.bfloat16)
        four = [s, s * x[0], s * x[1], s * x[2]]
        to_w[cell] = jnp.concatenate(four + four, axis=0)
        if to_i is not None:
            a, b, c = thirds(
                jnp.concatenate(
                    [-2.0 * x[0], -2.0 * x[1], -2.0 * x[2], one_row, norm, three_rows], axis=0
                )
            )
            ref, p, lane = to_i
            ref[p, :, TILE * lane : TILE * (lane + 1)] = jnp.concatenate(
                [a, b, a, b, c, a], axis=0
            ).astype(jnp.bfloat16)

    def prepare_pair(source, to_j, to_w, to_i, p):
        for lane in range(2):
            g = 2 * p + lane
            prepare(
                to_j,
                to_w,
                g + HALO,
                [source[d, pl.ds(g, 1), :] for d in range(3)],
                stg[pl.ds(g, 1), :],
                (to_i, p, lane),
            )

    def prepare_own(p, _):
        prepare_pair(pos, side_j, base_w, side_i, p)
        return 0

    lax.fori_loop(0, cells // 2, prepare_own, 0)
    for copy in loads[3:]:
        copy.wait()

    def prepare_halo(to_j, to_w, low, high):
        for k in range(HALO):
            for base, at, pos_of, str_of in (
                (0, 8 - HALO, low, low_s),
                (HALO + cells, 0, high, high_s),
            ):
                prepare(
                    to_j,
                    to_w,
                    base + k,
                    [pos_of[d, at + k : at + k + 1, :] for d in range(3)],
                    str_of[at + k : at + k + 1, :],
                )

    def force(of_j, of_i, of_w, source, p):
        weights = []
        for k in range(REACH + 1):
            parts = thirds(mult[k, p] * of_w[2 * p + k])
            weights.append(
                jnp.concatenate(list(parts) + [jnp.zeros((8, TILE), jnp.float32)], axis=0)
            )
        weights = jnp.concatenate(weights, axis=1).astype(jnp.bfloat16)
        keys_i = of_i[p]
        total = None
        for k in range((REACH + 1) // 2):
            highs, lows = [], []
            at = pl.multiple_of((p + k) * 2 * TILE, 2 * TILE)
            block = jnp.dot(
                of_j[pl.ds(at, 2 * TILE), :], keys_i, preferred_element_type=jnp.float32
            )
            for b in range(2 * TILE // CHUNK):
                q = block[CHUNK * b : CHUNK * (b + 1)]
                f = pltpu.reciprocal(q * q, approx=True)
                high = f.astype(jnp.bfloat16)
                highs.append(high)
                lows.append((f - high.astype(jnp.float32)).astype(jnp.bfloat16))
            w = weights[:, 2 * TILE * k : 2 * TILE * (k + 1)]
            for piece in (highs, lows):
                term = jnp.dot(
                    w, jnp.concatenate(piece, axis=0), preferred_element_type=jnp.float32
                )
                total = term if total is None else total + term
        total = total[0:8] + (total[8:16] + total[16:24])
        result = []
        for lane in range(2):
            g = 2 * p + lane
            part_of = total[4 * lane : 4 * lane + 4, TILE * lane : TILE * (lane + 1)]
            s = stg[pl.ds(g, 1), :]
            result.append(
                [
                    s * (source[d, pl.ds(g, 1), :] * part_of[0:1] - part_of[d + 1 : d + 2])
                    for d in range(3)
                ]
            )
        return result

    def stage_at(g):
        inner = g < near
        h = jnp.where(inner, g // 8, (g - near) // 4)
        base = jnp.where(inner, g % 8, SPLIT + (g - near) % 4)
        return h, base, jnp.where(inner, 8, 4)

    top = cells - 8
    halos = [
        remote(pos.at[:, pl.ds(top, 8), :], low_p, halo_send.at[0], halo_recv.at[0], right),
        remote(pos.at[:, pl.ds(0, 8), :], high_p, halo_send.at[1], halo_recv.at[1], left),
        remote(stg.at[pl.ds(top, 8), :], low_s, halo_send.at[2], halo_recv.at[2], right),
        remote(stg.at[pl.ds(0, 8), :], high_s, halo_send.at[3], halo_recv.at[3], left),
    ]
    nexts = [
        remote(x1.at[:, pl.ds(top, 8), :], low_n, halo_send.at[4], halo_recv.at[4], right),
        remote(x1.at[:, pl.ds(0, 8), :], high_n, halo_send.at[5], halo_recv.at[5], left),
    ]

    pairs = cells // 2

    def order_one(t):
        return (t + 1) % pairs

    def first_step(t, _):
        @pl.when(t == 2)
        def _():
            pl.semaphore_wait(barrier, (nx - 1) + (members - 1) + 2 * (n - 1))
            for copy in halos:
                copy.start()

        @pl.when(t == pairs - 2)
        def _():
            for copy in halos:
                copy.wait()
            prepare_halo(side_j, base_w, low_p, high_p)

        p = order_one(t)
        prepare_pair(x1, next_j, next_w, next_i, order_one(t + pairs - 1))
        f = force(side_j, side_i, base_w, pos, p)
        for lane in range(2):
            g = 2 * p + lane
            h, base, stride = stage_at(g)
            for d in range(3):
                v = vel[d, pl.ds(g, 1), :] + STEP * f[lane][d]
                x = pos[d, pl.ds(g, 1), :] + STEP * v
                v1[d, pl.ds(g, 1), :] = v
                x1[d, pl.ds(g, 1), :] = x
                stage_x[h, pl.ds(base + d * stride, 1), :] = x
        return 0

    lax.fori_loop(0, pairs, first_step, 0)
    for copy in nexts:
        copy.start()

    def spread_state(a, stage, held):
        for h, own, low, step in ((0, zz, 2 * yy, members), (1, yy, zz * members + 1, 2)):

            def send(p, h=h, own=own, low=low, step=step):
                remote(
                    stage.at[h],
                    held.at[2 * own + core],
                    one_send.at[a],
                    one_recv.at[a],
                    (low + p * step, here),
                ).start()

            others(n, own, send)
        remote(
            stage.at[pair],
            held.at[2 * second + core],
            one_send.at[a],
            one_recv.at[a],
            (twin, here),
        ).start()
        held[2 * first + core] = stage[core]

    def source_of(slot):
        row = home[plan[slot]]
        return lax.div(row, members), lax.rem(lax.div(row, 2), n), lax.rem(row, 2)

    slots, origins = [], []
    for q in range(n):
        for c in range(2):
            slot = first * first_stride + q * second_stride + c
            z, y, c_src = source_of(slot)
            slots.append(slot)
            origins.append(2 * (z + core * (y - z)) + c_src)

    def hand_on(a, held, pick, take):
        wait_all(held.at[pl.ds(0, members - 1)], one_recv.at[a])

        for k, (slot, origin) in enumerate(zip(slots, origins)):
            pick[k] = held[origin]

            @pl.when(slot != me)
            def _(slot=slot, k=k):
                remote(
                    pick.at[k],
                    take.at[core * n + second],
                    two_send.at[a],
                    two_recv.at[a],
                    (slot, here),
                ).start()

        take[core * n + second] = pick[2 * second + core]

    spread_state(0, stage_x, held_x)
    prepare_pair(x1, next_j, next_w, next_i, order_one(pairs - 1))

    def share_features():
        feat_in[mine] = feat[mine]
        wait_all(feat_in.at[pl.ds(0, members - 1)], feat_recv.at[0])
        for d in range(3):
            group[zz, :, TILE * d : TILE * (d + 1)] = feat_in[:, d, :].astype(jnp.bfloat16)
        others(
            n,
            zz,
            lambda z: remote(
                group.at[zz], group.at[zz], feat_send.at[1], feat_recv.at[1], level(z)
            ).start(),
        )

    near_pairs = near // 2

    def second_step(t, _):
        @pl.when(t == near_pairs - 1)
        def _():
            for copy in nexts:
                copy.wait()
            prepare_halo(next_j, next_w, low_n, high_n)

        @pl.when(t == near_pairs)
        def _():
            spread_state(1, stage_va, held_va)

        @pl.when(t == near_pairs + 1)
        def _():
            share_features()
            hand_on(0, held_x, pick_x, take_x)

        p = jnp.where(t < near_pairs, (t + 1) % near_pairs, t)
        f = force(next_j, next_i, next_w, x1, p)
        for lane in range(2):
            g = 2 * p + lane
            h, base, stride = stage_at(g)
            for d in range(3):
                v = v1[d, pl.ds(g, 1), :] + STEP * f[lane][d]
                x = x1[d, pl.ds(g, 1), :] + STEP * v

                @pl.when(t < near_pairs)
                def _(v=v, h=h, base=base, d=d):
                    stage_va[h, pl.ds(base + 8 * d, 1), :] = v

                @pl.when(t >= near_pairs)
                def _(v=v, h=h, base=base, d=d):
                    stage_vb[h, pl.ds(base - SPLIT + 4 * d, 1), :] = v

                feat[g, pl.ds(d, 1), :] = x

            @pl.when((g < members) & (g != mine))
            def _(g=g):
                remote(
                    feat.at[g], feat_in.at[mine], feat_send.at[0], feat_recv.at[0], member(g)
                ).start()

        return 0

    lax.fori_loop(0, pairs, second_step, 0)
    spread_state(2, stage_vb, held_vb)
    hand_on(1, held_va, pick_va, take_va)

    wait_all(group.at[pl.ds(0, n - 1)], feat_recv.at[1])
    wide[...] = group[...].astype(jnp.float32).reshape(walkers, 3 * TILE)
    for d in range(3):
        own_rows[d] = group[zz, :, TILE * d : TILE * (d + 1)].astype(jnp.float32)
    lanes = lax.broadcasted_iota(jnp.int32, (walkers, TILE), 1)

    def row_of(r, acc):
        total = None
        for d in range(3):
            diff = wide[:, TILE * d : TILE * (d + 1)] - own_rows[d, pl.ds(r, 1), :]
            square = diff * diff
            total = square if total is None else total + square
        return jnp.where(lanes == r, jnp.sum(total, axis=1, keepdims=True), acc)

    sums = lax.fori_loop(0, members, row_of, jnp.zeros((walkers, TILE), jnp.float32)).T
    for r in range(members):
        part[r, :, 0:walkers] = jnp.broadcast_to(sums[r : r + 1], (8, walkers))
    others(
        members,
        mine,
        lambda m: remote(
            part.at[m], part_in.at[mine], feat_send.at[2], feat_recv.at[2], member(m)
        ).start(),
    )
    part_in[mine] = part[mine]

    hand_on(2, held_vb, pick_vb, take_vb)

    wait_all(part_in.at[pl.ds(0, members - 1)], feat_recv.at[2])
    row = part_in[0]
    for m in range(1, members):
        row = row + part_in[m]
    line[here] = row
    others(
        nx,
        here,
        lambda s: remote(
            line.at[here], line.at[here], feat_send.at[3], feat_recv.at[3], (me, s)
        ).start(),
    )
    wait_all(line.at[pl.ds(0, nx - 1)], feat_recv.at[3])
    row = line[0, 0:1, 0:walkers]
    for s in range(1, nx):
        row = row + line[s, 0:1, 0:walkers]
    row = row / (3.0 * sites)
    share = walkers // nx
    mine_of = row[:, 0:share]
    for s in range(1, nx):
        mine_of = jnp.where(here == s, row[:, share * s : share * (s + 1)], mine_of)
    dist[...] = mine_of

    for a, take in enumerate((take_x, take_va, take_vb)):
        wait_all(take.at[pl.ds(0, members - 1)], two_recv.at[a])

    z, y, _ = source_of(me)
    for h, index in ((0, y), (1, n + z)):
        x = take_x[index]
        va = take_va[index]
        vb = take_vb[index]
        if h == 0:
            same = (planv[...] == plan[me]).astype(jnp.float32)
            nwt[...] = x[36:37, 0:1] / jnp.sum(same, axis=1, keepdims=True)
        xa = x[0:SPLIT] + STEP * va
        xb = x[SPLIT:ROWS] + STEP * vb
        for out, of_a, of_b in ((nvel, va, vb), (npos, xa, xb)):
            for d in range(3):
                out[d, 8 * h : 8 * h + 8, :] = of_a[8 * d : 8 * d + 8]
                out[d, near + 4 * h : near + 4 * h + 4, :] = of_b[4 * d : 4 * d + 4]

    for a, held in enumerate((held_x, held_va, held_vb)):
        wait_all(held.at[pl.ds(0, members - 1)], one_send.at[a])
        wait_all(held.at[pl.ds(0, members - 1)], two_send.at[a])
    wait_all(feat_in.at[pl.ds(0, members - 1)], feat_send.at[0])
    wait_all(group.at[pl.ds(0, n - 1)], feat_send.at[1])
    wait_all(part_in.at[pl.ds(0, members - 1)], feat_send.at[2])
    wait_all(line.at[pl.ds(0, nx - 1)], feat_send.at[3])


def solution(mesh):
    walkers = mesh.shape["walker"]
    nx = mesh.shape["space"]
    n = 1
    while 2 * n * n < walkers:
        n += 1
    members = 2 * n

    def shards(positions, velocities, weights, strength, tiles, plan, home):
        cells = tiles.shape[0]
        ext = cells + 2 * HALO
        f32 = jnp.float32
        vmem = pl.BlockSpec(memory_space=pltpu.VMEM)
        smem = pl.BlockSpec(memory_space=pltpu.SMEM)
        hbm = pl.BlockSpec(memory_space=pltpu.HBM)
        dma = pltpu.SemaphoreType.DMA
        block = jax.ShapeDtypeStruct((3, cells, TILE), f32)

        def pinned(x):
            return pltpu.with_memory_space_constraint(x, pltpu.HBM)

        def room(*shape, kind=f32):
            return pltpu.VMEM(shape, kind)

        dist, npos, nvel, nwt = pl.pallas_call(
            functools.partial(kernel, n, nx),
            out_shape=(
                jax.ShapeDtypeStruct((1, walkers // nx), f32),
                block,
                block,
                jax.ShapeDtypeStruct((1, 1), f32),
            ),
            in_specs=[hbm] * 7 + [smem],
            out_specs=(vmem,) * 4,
            scratch_shapes=[
                room(3, cells, TILE),
                room(3, cells, TILE),
                room(cells, TILE),
                room(*tiles.shape, kind=jnp.int32),
                room(1, walkers, kind=jnp.int32),
                pltpu.SMEM((walkers,), jnp.int32),
                pltpu.SMEM((walkers,), jnp.int32),
                room(ext * TILE, KEYS, kind=jnp.bfloat16),
                room(ext * TILE, KEYS, kind=jnp.bfloat16),
                room(cells // 2, KEYS, 2 * TILE, kind=jnp.bfloat16),
                room(cells // 2, KEYS, 2 * TILE, kind=jnp.bfloat16),
                room(ext, 8, TILE),
                room(ext, 8, TILE),
                room(REACH + 1, cells // 2, 8, TILE),
                room(3, cells, TILE),
                room(3, cells, TILE),
                room(3, 8, TILE),
                room(3, 8, TILE),
                room(8, TILE),
                room(8, TILE),
                room(3, 8, TILE),
                room(3, 8, TILE),
                room(2, ROWS, TILE),
                room(2, SPLIT, TILE),
                room(2, ROWS - SPLIT, TILE),
                room(cells, 8, TILE),
                room(members, 8, TILE),
                room(n, members, 3 * TILE, kind=jnp.bfloat16),
                room(walkers, 3 * TILE),
                room(3, members, TILE),
                room(members, 8, TILE),
                room(members, 8, TILE),
                room(nx, 8, TILE),
                room(members, ROWS, TILE),
                room(members, SPLIT, TILE),
                room(members, ROWS - SPLIT, TILE),
                room(members, ROWS, TILE),
                room(members, SPLIT, TILE),
                room(members, ROWS - SPLIT, TILE),
                room(members, ROWS, TILE),
                room(members, SPLIT, TILE),
                room(members, ROWS - SPLIT, TILE),
                dma((7,)),
                dma((6,)),
                dma((6,)),
                dma((4,)),
                dma((4,)),
                dma((3,)),
                dma((3,)),
                dma((3,)),
                dma((3,)),
            ],
            compiler_params=pltpu.CompilerParams(
                collective_id=0,
                has_side_effects=True,
                vmem_limit_bytes=40 * 1024 * 1024,
            ),
        )(
            pinned(positions.reshape(3, cells, TILE)),
            pinned(velocities.reshape(3, cells, TILE)),
            pinned(strength.reshape(cells, TILE)),
            pinned(tiles),
            pinned(plan.reshape(1, walkers)),
            pinned(plan),
            pinned(home),
            weights,
        )
        return (
            dist,
            npos.reshape(1, 3, cells * TILE),
            nvel.reshape(1, 3, cells * TILE),
            nwt.reshape(1),
        )

    return jax.shard_map(
        shards,
        mesh=mesh,
        in_specs=(
            P("walker", None, "space"),
            P("walker", None, "space"),
            P("walker"),
            P("space"),
            P("space", None),
            P(),
            P(),
        ),
        out_specs=(
            P("walker", "space"),
            P("walker", None, "space"),
            P("walker", None, "space"),
            P("walker"),
        ),
        check_vma=False,
    )
```

```python
import functools

import jax
import jax.numpy as jnp
from jax import lax
from jax.experimental import pallas as pl
from jax.experimental.pallas import tpu as pltpu
from jax.sharding import PartitionSpec as P

HALO = 2
REACH = 2 * HALO + 1
STEP = 0.1
TILE = 128
ROWS = 40
SPLIT = 24
KEYS = 48
CHUNK = 32
MESH = pl.DeviceIdType.MESH


def kernel(
    n,
    nx,
    pos_in,
    vel_in,
    stg_in,
    til_in,
    row_in,
    plan_in,
    home_in,
    wgt,
    dist,
    npos,
    nvel,
    nwt,
    pos,
    vel,
    stg,
    til,
    planv,
    plan,
    home,
    side_j,
    next_j,
    side_i,
    next_i,
    base_w,
    next_w,
    mult,
    x1,
    v1,
    low_p,
    high_p,
    low_s,
    high_s,
    low_n,
    high_n,
    stage_x,
    stage_va,
    stage_vb,
    feat,
    feat_in,
    group,
    wide,
    own_rows,
    part,
    part_in,
    line,
    held_x,
    held_va,
    held_vb,
    pick_x,
    pick_va,
    pick_vb,
    take_x,
    take_va,
    take_vb,
    load_sem,
    halo_send,
    halo_recv,
    feat_send,
    feat_recv,
    one_send,
    one_recv,
    two_send,
    two_recv,
    far_recv,
):
    cells = pos.shape[1]
    members = 2 * n
    walkers = members * n
    near = cells - 8
    sites = members * TILE * nx
    me = lax.axis_index("walker")
    here = lax.axis_index("space")
    core = me % 2
    yy = (me // 2) % n
    zz = me // members
    mine = me % members

    first = zz + core * (yy - zz)
    second = yy + core * (zz - yy)
    first_stride = 2 * (n - (n - 1) * core)
    second_stride = 2 * (1 + (n - 1) * core)
    pair = 1 - core
    twin = me + pair - core

    loads = [
        pltpu.make_async_copy(src, dst, load_sem.at[i])
        for i, (src, dst) in enumerate(
            ((pos_in, pos), (stg_in, stg), (til_in, til), (vel_in, vel), (row_in, planv), (plan_in, plan), (home_in, home))
        )
    ]
    for copy in loads:
        copy.start()

    def member(m):
        return (zz * members + m, here)

    def level(z):
        return (z * members + mine, here)

    right = (me, (here + 1) % nx)
    left = (me, (here + nx - 1) % nx)

    def others(count, own, act):
        for k in range(1, count):
            act(lax.rem(own + k, count))

    barrier = pltpu.get_barrier_semaphore()

    def hello(where):
        pl.semaphore_signal(barrier, inc=1, device_id=where, device_id_type=MESH)

    others(nx, here, lambda s: hello((me, s)))
    others(members, mine, lambda m: hello(member(m)))

    def hello_level(z):
        hello(level(z))
        hello((z * members + mine + pair - core, here))

    others(n, zz, hello_level)

    def remote(src, dst, send, recv, where):
        return pltpu.make_async_remote_copy(
            src_ref=src,
            dst_ref=dst,
            send_sem=send,
            recv_sem=recv,
            device_id=where,
            device_id_type=MESH,
        )

    def wait_all(ref, sem):
        pltpu.make_async_copy(ref, ref, sem).wait()

    for h in range(2):
        stage_x[h, pl.ds(36, 4), :] = jnp.broadcast_to(wgt[0], (4, TILE))
        stage_vb[h, pl.ds(12, 4), :] = jnp.zeros((4, TILE), jnp.float32)
    feat[...] = jnp.zeros(feat.shape, jnp.float32)
    x1[...] = jnp.zeros(x1.shape, jnp.float32)

    for copy in loads[:3]:
        copy.wait()

    shift = til[...] - lax.broadcasted_iota(jnp.int32, til.shape, 0)
    hits = [
        jnp.broadcast_to(
            jnp.sum((shift == o).astype(jnp.float32), axis=1, keepdims=True), (cells, TILE)
        )
        for o in range(REACH)
    ]
    none = jnp.zeros((4, TILE), jnp.float32)
    for k in range(REACH + 1):
        for p in range(cells // 2):
            for row, g, o in ((0, 2 * p, k), (4, 2 * p + 1, k - 1)):
                value = none
                if 0 <= o < REACH:
                    value = jnp.broadcast_to(hits[o][g : g + 1], (4, TILE))
                mult[k, p, row : row + 4, :] = value

    def thirds(x):
        high = x.astype(jnp.bfloat16).astype(jnp.float32)
        rest = x - high
        middle = rest.astype(jnp.bfloat16).astype(jnp.float32)
        return high, middle, rest - middle

    one_row = jnp.ones((1, TILE), jnp.float32)
    three_rows = jnp.zeros((3, TILE), jnp.float32)

    def prepare(to_j, to_w, cell, x, s, to_i=None):
        norm = x[0] * x[0] + x[1] * x[1] + x[2] * x[2]
        a, b, c = thirds(
            jnp.concatenate([x[0], x[1], x[2], norm + 1.0, one_row, three_rows], axis=0)
        )
        keys = jnp.concatenate([a, a, b, b, a, c], axis=0).T
        to_j[pl.ds(pl.multiple_of(cell * TILE, TILE), TILE), :] = keys.astype(jnp.bfloat16)
        four = [s, s * x[0], s * x[1], s * x[2]]
        to_w[cell] = jnp.concatenate(four + four, axis=0)
        if to_i is not None:
            a, b, c = thirds(
                jnp.concatenate(
                    [-2.0 * x[0], -2.0 * x[1], -2.0 * x[2], one_row, norm, three_rows], axis=0
                )
            )
            ref, p, lane = to_i
            ref[p, :, TILE * lane : TILE * (lane + 1)] = jnp.concatenate(
                [a, b, a, b, c, a], axis=0
            ).astype(jnp.bfloat16)

    def prepare_pair(source, to_j, to_w, to_i, p):
        for lane in range(2):
            g = 2 * p + lane
            prepare(
                to_j,
                to_w,
                g + HALO,
                [source[d, pl.ds(g, 1), :] for d in range(3)],
                stg[pl.ds(g, 1), :],
                (to_i, p, lane),
            )

    def prepare_own(p, _):
        prepare_pair(pos, side_j, base_w, side_i, p)
        return 0

    lax.fori_loop(0, cells // 2, prepare_own, 0)
    for copy in loads[3:]:
        copy.wait()

    def prepare_halo(to_j, to_w, low, high):
        for k in range(HALO):
            for base, at, pos_of, str_of in (
                (0, 8 - HALO, low, low_s),
                (HALO + cells, 0, high, high_s),
            ):
                prepare(
                    to_j,
                    to_w,
                    base + k,
                    [pos_of[d, at + k : at + k + 1, :] for d in range(3)],
                    str_of[at + k : at + k + 1, :],
                )

    def force(of_j, of_i, of_w, source, p):
        weights = []
        for k in range(REACH + 1):
            parts = thirds(mult[k, p] * of_w[2 * p + k])
            weights.append(
                jnp.concatenate(list(parts) + [jnp.zeros((8, TILE), jnp.float32)], axis=0)
            )
        weights = jnp.concatenate(weights, axis=1).astype(jnp.bfloat16)
        keys_i = of_i[p]
        total = None
        for k in range((REACH + 1) // 2):
            highs, lows = [], []
            at = pl.multiple_of((p + k) * 2 * TILE, 2 * TILE)
            block = jnp.dot(
                of_j[pl.ds(at, 2 * TILE), :], keys_i, preferred_element_type=jnp.float32
            )
            for b in range(2 * TILE // CHUNK):
                q = block[CHUNK * b : CHUNK * (b + 1)]
                f = pltpu.reciprocal(q * q, approx=True)
                high = f.astype(jnp.bfloat16)
                highs.append(high)
                lows.append((f - high.astype(jnp.float32)).astype(jnp.bfloat16))
            w = weights[:, 2 * TILE * k : 2 * TILE * (k + 1)]
            for piece in (highs, lows):
                term = jnp.dot(
                    w, jnp.concatenate(piece, axis=0), preferred_element_type=jnp.float32
                )
                total = term if total is None else total + term
        total = total[0:8] + (total[8:16] + total[16:24])
        result = []
        for lane in range(2):
            g = 2 * p + lane
            part_of = total[4 * lane : 4 * lane + 4, TILE * lane : TILE * (lane + 1)]
            s = stg[pl.ds(g, 1), :]
            result.append(
                [
                    s * (source[d, pl.ds(g, 1), :] * part_of[0:1] - part_of[d + 1 : d + 2])
                    for d in range(3)
                ]
            )
        return result

    def stage_at(g):
        inner = g < near
        h = jnp.where(inner, g // 8, (g - near) // 4)
        base = jnp.where(inner, g % 8, SPLIT + (g - near) % 4)
        return h, base, jnp.where(inner, 8, 4)

    top = cells - 8
    halos = [
        remote(pos.at[:, pl.ds(top, 8), :], low_p, halo_send.at[0], halo_recv.at[0], right),
        remote(pos.at[:, pl.ds(0, 8), :], high_p, halo_send.at[1], halo_recv.at[1], left),
        remote(stg.at[pl.ds(top, 8), :], low_s, halo_send.at[2], halo_recv.at[2], right),
        remote(stg.at[pl.ds(0, 8), :], high_s, halo_send.at[3], halo_recv.at[3], left),
    ]
    nexts = [
        remote(x1.at[:, pl.ds(top, 8), :], low_n, halo_send.at[4], halo_recv.at[4], right),
        remote(x1.at[:, pl.ds(0, 8), :], high_n, halo_send.at[5], halo_recv.at[5], left),
    ]

    pairs = cells // 2

    def order_one(t):
        return (t + 1) % pairs

    def first_step(t, _):
        @pl.when(t == 2)
        def _():
            pl.semaphore_wait(barrier, (nx - 1) + (members - 1) + 2 * (n - 1))
            for copy in halos:
                copy.start()

        @pl.when(t == pairs - 2)
        def _():
            for copy in halos:
                copy.wait()
            prepare_halo(side_j, base_w, low_p, high_p)

        p = order_one(t)
        prepare_pair(x1, next_j, next_w, next_i, order_one(t + pairs - 1))
        f = force(side_j, side_i, base_w, pos, p)
        for lane in range(2):
            g = 2 * p + lane
            h, base, stride = stage_at(g)
            for d in range(3):
                v = vel[d, pl.ds(g, 1), :] + STEP * f[lane][d]
                x = pos[d, pl.ds(g, 1), :] + STEP * v
                v1[d, pl.ds(g, 1), :] = v
                x1[d, pl.ds(g, 1), :] = x
                stage_x[h, pl.ds(base + d * stride, 1), :] = x
        return 0

    lax.fori_loop(0, pairs, first_step, 0)
    for copy in nexts:
        copy.start()

    relay = n == 8

    def spread_state(a, stage, held):
        for h, own, low, step in ((0, zz, 2 * yy, members), (1, yy, zz * members + 1, 2)):

            for k in (2, 6, 1, 7) if relay else range(1, n):
                p = lax.rem(own + k, n)
                remote(
                    stage.at[h],
                    held.at[2 * own + core],
                    one_send.at[a],
                    (far_recv if relay and k in (2, 6) else one_recv).at[a],
                    (low + p * step, here),
                ).start()
        remote(
            stage.at[pair],
            held.at[2 * second + core],
            one_send.at[a],
            one_recv.at[a],
            (twin, here),
        ).start()
        held[2 * first + core] = stage[core]

    def send_on(a, held):
        if not relay:
            return
        wait_all(held.at[pl.ds(0, 4)], far_recv.at[a])
        for away, near_step, c in ((2, 1, 0), (6, 7, 1)):
            back = lax.rem(first + n - away, n)
            for step, at, count in ((near_step, 2 * back, 2), (away, 2 * back + c, 1)):
                p = lax.rem(first + step, n)
                remote(
                    held.at[pl.ds(at, count)],
                    held.at[pl.ds(at, count)],
                    one_send.at[a],
                    one_recv.at[a],
                    (p * first_stride + second * second_stride + core, here),
                ).start()

    def source_of(slot):
        row = home[plan[slot]]
        return lax.div(row, members), lax.rem(lax.div(row, 2), n), lax.rem(row, 2)

    slots, origins = [], []
    for q in range(n):
        for c in range(2):
            slot = first * first_stride + q * second_stride + c
            z, y, c_src = source_of(slot)
            slots.append(slot)
            origins.append(2 * (z + core * (y - z)) + c_src)

    def hand_on(a, held, pick, take):
        wait_all(held.at[pl.ds(0, members - (5 if relay else 1))], one_recv.at[a])

        for k, (slot, origin) in enumerate(zip(slots, origins)):
            pick[k] = held[origin]

            @pl.when(slot != me)
            def _(slot=slot, k=k):
                remote(
                    pick.at[k],
                    take.at[core * n + second],
                    two_send.at[a],
                    two_recv.at[a],
                    (slot, here),
                ).start()

        take[core * n + second] = pick[2 * second + core]

    spread_state(0, stage_x, held_x)
    prepare_pair(x1, next_j, next_w, next_i, order_one(pairs - 1))

    def share_features():
        feat_in[mine] = feat[mine]
        wait_all(feat_in.at[pl.ds(0, members - 1)], feat_recv.at[0])
        for d in range(3):
            group[zz, :, TILE * d : TILE * (d + 1)] = feat_in[:, d, :].astype(jnp.bfloat16)
        others(
            n,
            zz,
            lambda z: remote(
                group.at[zz], group.at[zz], feat_send.at[1], feat_recv.at[1], level(z)
            ).start(),
        )

    near_pairs = near // 2

    def second_step(t, _):
        @pl.when(t == near_pairs - 1)
        def _():
            for copy in nexts:
                copy.wait()
            prepare_halo(next_j, next_w, low_n, high_n)

        @pl.when(t == near_pairs)
        def _():
            spread_state(1, stage_va, held_va)

        @pl.when(t == near_pairs + 1)
        def _():
            share_features()
            hand_on(0, held_x, pick_x, take_x)

        @pl.when(t == 4)
        def _():
            send_on(0, held_x)

        @pl.when(t == pairs - 1)
        def _():
            send_on(1, held_va)

        p = jnp.where(t < near_pairs, (t + 1) % near_pairs, t)
        f = force(next_j, next_i, next_w, x1, p)
        for lane in range(2):
            g = 2 * p + lane
            h, base, stride = stage_at(g)
            for d in range(3):
                v = v1[d, pl.ds(g, 1), :] + STEP * f[lane][d]
                x = x1[d, pl.ds(g, 1), :] + STEP * v

                @pl.when(t < near_pairs)
                def _(v=v, h=h, base=base, d=d):
                    stage_va[h, pl.ds(base + 8 * d, 1), :] = v

                @pl.when(t >= near_pairs)
                def _(v=v, h=h, base=base, d=d):
                    stage_vb[h, pl.ds(base - SPLIT + 4 * d, 1), :] = v

                feat[g, pl.ds(d, 1), :] = x

            @pl.when((g < members) & (g != mine))
            def _(g=g):
                remote(
                    feat.at[g], feat_in.at[mine], feat_send.at[0], feat_recv.at[0], member(g)
                ).start()

        return 0

    lax.fori_loop(0, pairs, second_step, 0)
    spread_state(2, stage_vb, held_vb)
    hand_on(1, held_va, pick_va, take_va)
    send_on(2, held_vb)

    wait_all(group.at[pl.ds(0, n - 1)], feat_recv.at[1])
    wide[...] = group[...].astype(jnp.float32).reshape(walkers, 3 * TILE)
    for d in range(3):
        own_rows[d] = group[zz, :, TILE * d : TILE * (d + 1)].astype(jnp.float32)
    lanes = lax.broadcasted_iota(jnp.int32, (walkers, TILE), 1)

    def row_of(r, acc):
        total = None
        for d in range(3):
            diff = wide[:, TILE * d : TILE * (d + 1)] - own_rows[d, pl.ds(r, 1), :]
            square = diff * diff
            total = square if total is None else total + square
        return jnp.where(lanes == r, jnp.sum(total, axis=1, keepdims=True), acc)

    sums = lax.fori_loop(0, members, row_of, jnp.zeros((walkers, TILE), jnp.float32)).T
    for r in range(members):
        part[r, :, 0:walkers] = sums[r : r + 1]
    others(
        members,
        mine,
        lambda m: remote(
            part.at[m], part_in.at[mine], feat_send.at[2], feat_recv.at[2], member(m)
        ).start(),
    )
    part_in[mine] = part[mine]

    hand_on(2, held_vb, pick_vb, take_vb)

    wait_all(part_in.at[pl.ds(0, members - 1)], feat_recv.at[2])
    row = part_in[0]
    for m in range(1, members):
        row = row + part_in[m]
    line[here] = row
    others(
        nx,
        here,
        lambda s: remote(
            line.at[here], line.at[here], feat_send.at[3], feat_recv.at[3], (me, s)
        ).start(),
    )
    wait_all(line.at[pl.ds(0, nx - 1)], feat_recv.at[3])
    row = line[0, 0:1, 0:walkers]
    for s in range(1, nx):
        row = row + line[s, 0:1, 0:walkers]
    row = row / (3.0 * sites)
    share = walkers // nx
    mine_of = row[:, 0:share]
    for s in range(1, nx):
        mine_of = jnp.where(here == s, row[:, share * s : share * (s + 1)], mine_of)
    dist[...] = mine_of

    for a, take in enumerate((take_x, take_va, take_vb)):
        wait_all(take.at[pl.ds(0, members - 1)], two_recv.at[a])

    z, y, _ = source_of(me)
    for h, index in ((0, y), (1, n + z)):
        x = take_x[index]
        va = take_va[index]
        vb = take_vb[index]
        if h == 0:
            same = (planv[...] == plan[me]).astype(jnp.float32)
            nwt[...] = x[36:37, 0:1] / jnp.sum(same, axis=1, keepdims=True)
        xa = x[0:SPLIT] + STEP * va
        xb = x[SPLIT:ROWS] + STEP * vb
        for out, of_a, of_b in ((nvel, va, vb), (npos, xa, xb)):
            for d in range(3):
                out[d, 8 * h : 8 * h + 8, :] = of_a[8 * d : 8 * d + 8]
                out[d, near + 4 * h : near + 4 * h + 4, :] = of_b[4 * d : 4 * d + 4]

    for a, held in enumerate((held_x, held_va, held_vb)):
        wait_all(held.at[pl.ds(0, members - 1)], one_send.at[a])
        wait_all(held.at[pl.ds(0, members - 1)], two_send.at[a])
    wait_all(feat_in.at[pl.ds(0, members - 1)], feat_send.at[0])
    wait_all(group.at[pl.ds(0, n - 1)], feat_send.at[1])
    wait_all(part_in.at[pl.ds(0, members - 1)], feat_send.at[2])
    wait_all(line.at[pl.ds(0, nx - 1)], feat_send.at[3])


def solution(mesh):
    walkers = mesh.shape["walker"]
    nx = mesh.shape["space"]
    n = 1
    while 2 * n * n < walkers:
        n += 1
    members = 2 * n

    def shards(positions, velocities, weights, strength, tiles, plan, home):
        cells = tiles.shape[0]
        ext = cells + 2 * HALO
        f32 = jnp.float32
        vmem = pl.BlockSpec(memory_space=pltpu.VMEM)
        smem = pl.BlockSpec(memory_space=pltpu.SMEM)
        hbm = pl.BlockSpec(memory_space=pltpu.HBM)
        dma = pltpu.SemaphoreType.DMA
        block = jax.ShapeDtypeStruct((3, cells, TILE), f32)

        def pinned(x):
            return pltpu.with_memory_space_constraint(x, pltpu.HBM)

        def room(*shape, kind=f32):
            return pltpu.VMEM(shape, kind)

        dist, npos, nvel, nwt = pl.pallas_call(
            functools.partial(kernel, n, nx),
            out_shape=(
                jax.ShapeDtypeStruct((1, walkers // nx), f32),
                block,
                block,
                jax.ShapeDtypeStruct((1, 1), f32),
            ),
            in_specs=[hbm] * 7 + [smem],
            out_specs=(vmem,) * 4,
            scratch_shapes=[
                room(3, cells, TILE),
                room(3, cells, TILE),
                room(cells, TILE),
                room(*tiles.shape, kind=jnp.int32),
                room(1, walkers, kind=jnp.int32),
                pltpu.SMEM((walkers,), jnp.int32),
                pltpu.SMEM((walkers,), jnp.int32),
                room(ext * TILE, KEYS, kind=jnp.bfloat16),
                room(ext * TILE, KEYS, kind=jnp.bfloat16),
                room(cells // 2, KEYS, 2 * TILE, kind=jnp.bfloat16),
                room(cells // 2, KEYS, 2 * TILE, kind=jnp.bfloat16),
                room(ext, 8, TILE),
                room(ext, 8, TILE),
                room(REACH + 1, cells // 2, 8, TILE),
                room(3, cells, TILE),
                room(3, cells, TILE),
                room(3, 8, TILE),
                room(3, 8, TILE),
                room(8, TILE),
                room(8, TILE),
                room(3, 8, TILE),
                room(3, 8, TILE),
                room(2, ROWS, TILE),
                room(2, SPLIT, TILE),
                room(2, ROWS - SPLIT, TILE),
                room(cells, 4, TILE),
                room(members, 4, TILE),
                room(n, members, 3 * TILE, kind=jnp.bfloat16),
                room(walkers, 3 * TILE),
                room(3, members, TILE),
                room(members, 1, TILE),
                room(members, 1, TILE),
                room(nx, 1, TILE),
                room(members, ROWS, TILE),
                room(members, SPLIT, TILE),
                room(members, ROWS - SPLIT, TILE),
                room(members, ROWS, TILE),
                room(members, SPLIT, TILE),
                room(members, ROWS - SPLIT, TILE),
                room(members, ROWS, TILE),
                room(members, SPLIT, TILE),
                room(members, ROWS - SPLIT, TILE),
                dma((7,)),
                dma((6,)),
                dma((6,)),
                dma((4,)),
                dma((4,)),
                dma((3,)),
                dma((3,)),
                dma((3,)),
                dma((3,)),
                dma((3,)),
            ],
            compiler_params=pltpu.CompilerParams(
                collective_id=0,
                has_side_effects=True,
                vmem_limit_bytes=40 * 1024 * 1024,
            ),
        )(
            pinned(positions.reshape(3, cells, TILE)),
            pinned(velocities.reshape(3, cells, TILE)),
            pinned(strength.reshape(cells, TILE)),
            pinned(tiles),
            pinned(plan.reshape(1, walkers)),
            pinned(plan),
            pinned(home),
            weights,
        )
        return (
            dist,
            npos.reshape(1, 3, cells * TILE),
            nvel.reshape(1, 3, cells * TILE),
            nwt.reshape(1),
        )

    return jax.shard_map(
        shards,
        mesh=mesh,
        in_specs=(
            P("walker", None, "space"),
            P("walker", None, "space"),
            P("walker"),
            P("space"),
            P("space", None),
            P(),
            P(),
        ),
        out_specs=(
            P("walker", "space"),
            P("walker", None, "space"),
            P("walker", None, "space"),
            P("walker"),
        ),
        check_vma=False,
    )
```

```python
import functools

import jax
import jax.numpy as jnp
from jax import lax
from jax.experimental import pallas as pl
from jax.experimental.pallas import tpu as pltpu
from jax.sharding import PartitionSpec as P

HALO = 2
REACH = 2 * HALO + 1
STEP = 0.1
TILE = 128
ROWS = 40
SPLIT = 24
KEYS = 48
CHUNK = 32
MESH = pl.DeviceIdType.MESH


def kernel(
    n,
    nx,
    pos_in,
    vel_in,
    stg_in,
    til_in,
    row_in,
    plan_in,
    home_in,
    wgt,
    dist,
    npos,
    nvel,
    nwt,
    pos,
    vel,
    stg,
    til,
    planv,
    plan,
    home,
    side_j,
    next_j,
    side_i,
    next_i,
    base_w,
    next_w,
    mult,
    x1,
    v1,
    low_p,
    high_p,
    low_s,
    high_s,
    low_n,
    high_n,
    stage_x,
    stage_va,
    stage_vb,
    feat,
    feat_in,
    group,
    wide,
    own_rows,
    part,
    part_in,
    line,
    held_x,
    held_va,
    held_vb,
    pick_x,
    pick_va,
    pick_vb,
    take_x,
    take_va,
    take_vb,
    load_sem,
    halo_send,
    halo_recv,
    feat_send,
    feat_recv,
    one_send,
    one_recv,
    two_send,
    two_recv,
):
    cells = pos.shape[1]
    members = 2 * n
    walkers = members * n
    near = cells - 8
    sites = members * TILE * nx
    me = lax.axis_index("walker")
    here = lax.axis_index("space")
    core = me % 2
    yy = (me // 2) % n
    zz = me // members
    mine = me % members

    first = zz + core * (yy - zz)
    second = yy + core * (zz - yy)
    first_stride = 2 * (n - (n - 1) * core)
    second_stride = 2 * (1 + (n - 1) * core)
    pair = 1 - core
    twin = me + pair - core

    loads = [
        pltpu.make_async_copy(src, dst, load_sem.at[i])
        for i, (src, dst) in enumerate(
            ((pos_in, pos), (stg_in, stg), (til_in, til), (vel_in, vel), (row_in, planv), (plan_in, plan), (home_in, home))
        )
    ]
    for copy in loads:
        copy.start()

    def member(m):
        return (zz * members + m, here)

    def level(z):
        return (z * members + mine, here)

    right = (me, (here + 1) % nx)
    left = (me, (here + nx - 1) % nx)

    def others(count, own, act):
        for k in range(1, count):
            act(lax.rem(own + k, count))

    barrier = pltpu.get_barrier_semaphore()

    def hello(where):
        pl.semaphore_signal(barrier, inc=1, device_id=where, device_id_type=MESH)

    others(nx, here, lambda s: hello((me, s)))
    others(members, mine, lambda m: hello(member(m)))

    def hello_level(z):
        hello(level(z))
        hello((z * members + mine + pair - core, here))

    others(n, zz, hello_level)

    def remote(src, dst, send, recv, where):
        return pltpu.make_async_remote_copy(
            src_ref=src,
            dst_ref=dst,
            send_sem=send,
            recv_sem=recv,
            device_id=where,
            device_id_type=MESH,
        )

    def wait_all(ref, sem):
        pltpu.make_async_copy(ref, ref, sem).wait()

    for h in range(2):
        stage_x[h, pl.ds(36, 4), :] = jnp.broadcast_to(wgt[0], (4, TILE))
        stage_vb[h, pl.ds(12, 4), :] = jnp.zeros((4, TILE), jnp.float32)
    feat[...] = jnp.zeros(feat.shape, jnp.float32)
    x1[...] = jnp.zeros(x1.shape, jnp.float32)

    for copy in loads[:3]:
        copy.wait()

    shift = til[...] - lax.broadcasted_iota(jnp.int32, til.shape, 0)
    hits = [
        jnp.broadcast_to(
            jnp.sum((shift == o).astype(jnp.float32), axis=1, keepdims=True), (cells, TILE)
        )
        for o in range(REACH)
    ]
    none = jnp.zeros((4, TILE), jnp.float32)
    for k in range(REACH + 1):
        for p in range(cells // 2):
            for row, g, o in ((0, 2 * p, k), (4, 2 * p + 1, k - 1)):
                value = none
                if 0 <= o < REACH:
                    value = jnp.broadcast_to(hits[o][g : g + 1], (4, TILE))
                mult[k, p, row : row + 4, :] = value

    def thirds(x):
        high = x.astype(jnp.bfloat16).astype(jnp.float32)
        rest = x - high
        middle = rest.astype(jnp.bfloat16).astype(jnp.float32)
        return high, middle, rest - middle

    one_row = jnp.ones((1, TILE), jnp.float32)
    three_rows = jnp.zeros((3, TILE), jnp.float32)

    def prepare(to_j, to_w, cell, x, s, to_i=None):
        norm = x[0] * x[0] + x[1] * x[1] + x[2] * x[2]
        a, b, c = thirds(
            jnp.concatenate([x[0], x[1], x[2], norm + 1.0, one_row, three_rows], axis=0)
        )
        keys = jnp.concatenate([a, a, b, b, a, c], axis=0).T
        to_j[pl.ds(pl.multiple_of(cell * TILE, TILE), TILE), :] = keys.astype(jnp.bfloat16)
        four = [s, s * x[0], s * x[1], s * x[2]]
        to_w[cell] = jnp.concatenate(four + four, axis=0)
        if to_i is not None:
            a, b, c = thirds(
                jnp.concatenate(
                    [-2.0 * x[0], -2.0 * x[1], -2.0 * x[2], one_row, norm, three_rows], axis=0
                )
            )
            ref, p, lane = to_i
            ref[p, :, TILE * lane : TILE * (lane + 1)] = jnp.concatenate(
                [a, b, a, b, c, a], axis=0
            ).astype(jnp.bfloat16)

    def prepare_pair(source, to_j, to_w, to_i, p):
        for lane in range(2):
            g = 2 * p + lane
            prepare(
                to_j,
                to_w,
                g + HALO,
                [source[d, pl.ds(g, 1), :] for d in range(3)],
                stg[pl.ds(g, 1), :],
                (to_i, p, lane),
            )

    def prepare_own(p, _):
        prepare_pair(pos, side_j, base_w, side_i, p)
        return 0

    lax.fori_loop(0, cells // 2, prepare_own, 0, unroll=4)
    for copy in loads[3:]:
        copy.wait()

    def prepare_halo(to_j, to_w, low, high):
        for k in range(HALO):
            for base, at, pos_of, str_of in (
                (0, 8 - HALO, low, low_s),
                (HALO + cells, 0, high, high_s),
            ):
                prepare(
                    to_j,
                    to_w,
                    base + k,
                    [pos_of[d, at + k : at + k + 1, :] for d in range(3)],
                    str_of[at + k : at + k + 1, :],
                )

    def force(of_j, of_i, of_w, source, p):
        weights = []
        for k in range(REACH + 1):
            parts = thirds(mult[k, p] * of_w[2 * p + k])
            weights.append(
                jnp.concatenate(list(parts) + [jnp.zeros((8, TILE), jnp.float32)], axis=0)
            )
        weights = jnp.concatenate(weights, axis=1).astype(jnp.bfloat16)
        keys_i = of_i[p]
        total = None
        for k in range((REACH + 1) // 2):
            highs, lows = [], []
            at = pl.multiple_of((p + k) * 2 * TILE, 2 * TILE)
            block = jnp.dot(
                of_j[pl.ds(at, 2 * TILE), :], keys_i, preferred_element_type=jnp.float32
            )
            for b in range(2 * TILE // CHUNK):
                q = block[CHUNK * b : CHUNK * (b + 1)]
                f = pltpu.reciprocal(q * q, approx=True)
                high = f.astype(jnp.bfloat16)
                highs.append(high)
                lows.append((f - high.astype(jnp.float32)).astype(jnp.bfloat16))
            w = weights[:, 2 * TILE * k : 2 * TILE * (k + 1)]
            for piece in (highs, lows):
                term = jnp.dot(
                    w, jnp.concatenate(piece, axis=0), preferred_element_type=jnp.float32
                )
                total = term if total is None else total + term
        total = total[0:8] + (total[8:16] + total[16:24])
        result = []
        for lane in range(2):
            g = 2 * p + lane
            part_of = total[4 * lane : 4 * lane + 4, TILE * lane : TILE * (lane + 1)]
            s = stg[pl.ds(g, 1), :]
            result.append(
                [
                    s * (source[d, pl.ds(g, 1), :] * part_of[0:1] - part_of[d + 1 : d + 2])
                    for d in range(3)
                ]
            )
        return result

    def stage_at(g):
        inner = g < near
        h = jnp.where(inner, g // 8, (g - near) // 4)
        base = jnp.where(inner, g % 8, SPLIT + (g - near) % 4)
        return h, base, jnp.where(inner, 8, 4)

    top = cells - 8
    halos = [
        remote(pos.at[:, pl.ds(top, 8), :], low_p, halo_send.at[0], halo_recv.at[0], right),
        remote(pos.at[:, pl.ds(0, 8), :], high_p, halo_send.at[1], halo_recv.at[1], left),
        remote(stg.at[pl.ds(top, 8), :], low_s, halo_send.at[2], halo_recv.at[2], right),
        remote(stg.at[pl.ds(0, 8), :], high_s, halo_send.at[3], halo_recv.at[3], left),
    ]
    nexts = [
        remote(x1.at[:, pl.ds(top, 8), :], low_n, halo_send.at[4], halo_recv.at[4], right),
        remote(x1.at[:, pl.ds(0, 8), :], high_n, halo_send.at[5], halo_recv.at[5], left),
    ]

    pairs = cells // 2

    def order_one(t):
        return (t + 1) % pairs

    def first_step(u, _):
        @pl.when(u == 1)
        def _():
            pl.semaphore_wait(barrier, (nx - 1) + (members - 1) + 2 * (n - 1))
            for copy in halos:
                copy.start()

        @pl.when(u == pairs // 2 - 1)
        def _():
            for copy in halos:
                copy.wait()
            prepare_halo(side_j, base_w, low_p, high_p)

        now = [order_one(2 * u + k) for k in range(2)]
        for k in range(2):
            prepare_pair(x1, next_j, next_w, next_i, order_one(2 * u + k + pairs - 2))
        both = [force(side_j, side_i, base_w, pos, p) for p in now]
        for p, f in zip(now, both):
            for lane in range(2):
                g = 2 * p + lane
                h, base, stride = stage_at(g)
                for d in range(3):
                    v = vel[d, pl.ds(g, 1), :] + STEP * f[lane][d]
                    x = pos[d, pl.ds(g, 1), :] + STEP * v
                    v1[d, pl.ds(g, 1), :] = v
                    x1[d, pl.ds(g, 1), :] = x
                    stage_x[h, pl.ds(base + d * stride, 1), :] = x
        return 0

    lax.fori_loop(0, pairs // 2, first_step, 0)
    for copy in nexts:
        copy.start()

    def spread_state(a, stage, held):
        for h, own, low, step in ((0, zz, 2 * yy, members), (1, yy, zz * members + 1, 2)):

            def send(p, h=h, own=own, low=low, step=step):
                remote(
                    stage.at[h],
                    held.at[2 * own + core],
                    one_send.at[a],
                    one_recv.at[a],
                    (low + p * step, here),
                ).start()

            others(n, own, send)
        remote(
            stage.at[pair],
            held.at[2 * second + core],
            one_send.at[a],
            one_recv.at[a],
            (twin, here),
        ).start()
        held[2 * first + core] = stage[core]

    def source_of(slot):
        row = home[plan[slot]]
        return lax.div(row, members), lax.rem(lax.div(row, 2), n), lax.rem(row, 2)

    slots, origins = [], []
    for q in range(n):
        for c in range(2):
            slot = first * first_stride + q * second_stride + c
            z, y, c_src = source_of(slot)
            slots.append(slot)
            origins.append(2 * (z + core * (y - z)) + c_src)

    def hand_on(a, held, pick, take):
        wait_all(held.at[pl.ds(0, members - 1)], one_recv.at[a])

        for k, (slot, origin) in enumerate(zip(slots, origins)):
            pick[k] = held[origin]

            @pl.when(slot != me)
            def _(slot=slot, k=k):
                remote(
                    pick.at[k],
                    take.at[core * n + second],
                    two_send.at[a],
                    two_recv.at[a],
                    (slot, here),
                ).start()

        take[core * n + second] = pick[2 * second + core]

    spread_state(0, stage_x, held_x)
    for k in range(2):
        prepare_pair(x1, next_j, next_w, next_i, order_one(pairs - 2 + k))

    def share_features():
        feat_in[mine] = feat[mine]
        wait_all(feat_in.at[pl.ds(0, members - 1)], feat_recv.at[0])
        for d in range(3):
            group[zz, :, TILE * d : TILE * (d + 1)] = feat_in[:, d, :].astype(jnp.bfloat16)
        others(
            n,
            zz,
            lambda z: remote(
                group.at[zz], group.at[zz], feat_send.at[1], feat_recv.at[1], level(z)
            ).start(),
        )

    near_pairs = near // 2

    def second_step(u, _):
        @pl.when(u == near_pairs // 2 - 1)
        def _():
            for copy in nexts:
                copy.wait()
            prepare_halo(next_j, next_w, low_n, high_n)

        @pl.when(u == near_pairs // 2)
        def _():
            spread_state(1, stage_va, held_va)

        @pl.when(u == near_pairs // 2 + 1)
        def _():
            share_features()
            hand_on(0, held_x, pick_x, take_x)

        now = []
        for k in range(2):
            t = 2 * u + k
            now.append(jnp.where(t < near_pairs, (t + 1) % near_pairs, t))
        both = [force(next_j, next_i, next_w, x1, p) for p in now]
        rows = []
        for p, f in zip(now, both):
            for lane in range(2):
                g = 2 * p + lane
                h, base, _ = stage_at(g)
                for d in range(3):
                    v = v1[d, pl.ds(g, 1), :] + STEP * f[lane][d]
                    feat[g, pl.ds(d, 1), :] = x1[d, pl.ds(g, 1), :] + STEP * v
                    rows.append((h, base, d, v))

        @pl.when(u < near_pairs // 2)
        def _():
            for h, base, d, v in rows:
                stage_va[h, pl.ds(base + 8 * d, 1), :] = v

        @pl.when(u >= near_pairs // 2)
        def _():
            for h, base, d, v in rows:
                stage_vb[h, pl.ds(base - SPLIT + 4 * d, 1), :] = v

        for p in now:
            for lane in range(2):
                g = 2 * p + lane

                @pl.when((g < members) & (g != mine))
                def _(g=g):
                    remote(
                        feat.at[g], feat_in.at[mine], feat_send.at[0], feat_recv.at[0], member(g)
                    ).start()

        return 0

    lax.fori_loop(0, pairs // 2, second_step, 0)
    spread_state(2, stage_vb, held_vb)
    hand_on(1, held_va, pick_va, take_va)

    wait_all(group.at[pl.ds(0, n - 1)], feat_recv.at[1])
    wide[...] = group[...].astype(jnp.float32).reshape(walkers, 3 * TILE)
    for d in range(3):
        own_rows[d] = group[zz, :, TILE * d : TILE * (d + 1)].astype(jnp.float32)
    lanes = lax.broadcasted_iota(jnp.int32, (walkers, TILE), 1)

    def row_of(r, acc):
        total = None
        for d in range(3):
            diff = wide[:, TILE * d : TILE * (d + 1)] - own_rows[d, pl.ds(r, 1), :]
            square = diff * diff
            total = square if total is None else total + square
        return jnp.where(lanes == r, jnp.sum(total, axis=1, keepdims=True), acc)

    sums = lax.fori_loop(0, members, row_of, jnp.zeros((walkers, TILE), jnp.float32)).T
    for r in range(members):
        part[r, :, 0:walkers] = jnp.broadcast_to(sums[r : r + 1], (8, walkers))
    others(
        members,
        mine,
        lambda m: remote(
            part.at[m], part_in.at[mine], feat_send.at[2], feat_recv.at[2], member(m)
        ).start(),
    )
    part_in[mine] = part[mine]

    hand_on(2, held_vb, pick_vb, take_vb)

    wait_all(part_in.at[pl.ds(0, members - 1)], feat_recv.at[2])
    row = part_in[0]
    for m in range(1, members):
        row = row + part_in[m]
    line[here] = row
    others(
        nx,
        here,
        lambda s: remote(
            line.at[here], line.at[here], feat_send.at[3], feat_recv.at[3], (me, s)
        ).start(),
    )
    wait_all(line.at[pl.ds(0, nx - 1)], feat_recv.at[3])
    row = line[0, 0:1, 0:walkers]
    for s in range(1, nx):
        row = row + line[s, 0:1, 0:walkers]
    row = row / (3.0 * sites)
    share = walkers // nx
    mine_of = row[:, 0:share]
    for s in range(1, nx):
        mine_of = jnp.where(here == s, row[:, share * s : share * (s + 1)], mine_of)
    dist[...] = mine_of

    for a, take in enumerate((take_x, take_va, take_vb)):
        wait_all(take.at[pl.ds(0, members - 1)], two_recv.at[a])

    z, y, _ = source_of(me)
    for h, index in ((0, y), (1, n + z)):
        x = take_x[index]
        va = take_va[index]
        vb = take_vb[index]
        if h == 0:
            same = (planv[...] == plan[me]).astype(jnp.float32)
            nwt[...] = x[36:37, 0:1] / jnp.sum(same, axis=1, keepdims=True)
        xa = x[0:SPLIT] + STEP * va
        xb = x[SPLIT:ROWS] + STEP * vb
        for out, of_a, of_b in ((nvel, va, vb), (npos, xa, xb)):
            for d in range(3):
                out[d, 8 * h : 8 * h + 8, :] = of_a[8 * d : 8 * d + 8]
                out[d, near + 4 * h : near + 4 * h + 4, :] = of_b[4 * d : 4 * d + 4]

    for a, held in enumerate((held_x, held_va, held_vb)):
        wait_all(held.at[pl.ds(0, members - 1)], one_send.at[a])
        wait_all(held.at[pl.ds(0, members - 1)], two_send.at[a])
    wait_all(feat_in.at[pl.ds(0, members - 1)], feat_send.at[0])
    wait_all(group.at[pl.ds(0, n - 1)], feat_send.at[1])
    wait_all(part_in.at[pl.ds(0, members - 1)], feat_send.at[2])
    wait_all(line.at[pl.ds(0, nx - 1)], feat_send.at[3])


def solution(mesh):
    walkers = mesh.shape["walker"]
    nx = mesh.shape["space"]
    n = 1
    while 2 * n * n < walkers:
        n += 1
    members = 2 * n

    def shards(positions, velocities, weights, strength, tiles, plan, home):
        cells = tiles.shape[0]
        ext = cells + 2 * HALO
        f32 = jnp.float32
        vmem = pl.BlockSpec(memory_space=pltpu.VMEM)
        smem = pl.BlockSpec(memory_space=pltpu.SMEM)
        hbm = pl.BlockSpec(memory_space=pltpu.HBM)
        dma = pltpu.SemaphoreType.DMA
        block = jax.ShapeDtypeStruct((3, cells, TILE), f32)

        def pinned(x):
            return pltpu.with_memory_space_constraint(x, pltpu.HBM)

        def room(*shape, kind=f32):
            return pltpu.VMEM(shape, kind)

        dist, npos, nvel, nwt = pl.pallas_call(
            functools.partial(kernel, n, nx),
            out_shape=(
                jax.ShapeDtypeStruct((1, walkers // nx), f32),
                block,
                block,
                jax.ShapeDtypeStruct((1, 1), f32),
            ),
            in_specs=[hbm] * 7 + [smem],
            out_specs=(vmem,) * 4,
            scratch_shapes=[
                room(3, cells, TILE),
                room(3, cells, TILE),
                room(cells, TILE),
                room(*tiles.shape, kind=jnp.int32),
                room(1, walkers, kind=jnp.int32),
                pltpu.SMEM((walkers,), jnp.int32),
                pltpu.SMEM((walkers,), jnp.int32),
                room(ext * TILE, KEYS, kind=jnp.bfloat16),
                room(ext * TILE, KEYS, kind=jnp.bfloat16),
                room(cells // 2, KEYS, 2 * TILE, kind=jnp.bfloat16),
                room(cells // 2, KEYS, 2 * TILE, kind=jnp.bfloat16),
                room(ext, 8, TILE),
                room(ext, 8, TILE),
                room(REACH + 1, cells // 2, 8, TILE),
                room(3, cells, TILE),
                room(3, cells, TILE),
                room(3, 8, TILE),
                room(3, 8, TILE),
                room(8, TILE),
                room(8, TILE),
                room(3, 8, TILE),
                room(3, 8, TILE),
                room(2, ROWS, TILE),
                room(2, SPLIT, TILE),
                room(2, ROWS - SPLIT, TILE),
                room(cells, 8, TILE),
                room(members, 8, TILE),
                room(n, members, 3 * TILE, kind=jnp.bfloat16),
                room(walkers, 3 * TILE),
                room(3, members, TILE),
                room(members, 8, TILE),
                room(members, 8, TILE),
                room(nx, 8, TILE),
                room(members, ROWS, TILE),
                room(members, SPLIT, TILE),
                room(members, ROWS - SPLIT, TILE),
                room(members, ROWS, TILE),
                room(members, SPLIT, TILE),
                room(members, ROWS - SPLIT, TILE),
                room(members, ROWS, TILE),
                room(members, SPLIT, TILE),
                room(members, ROWS - SPLIT, TILE),
                dma((7,)),
                dma((6,)),
                dma((6,)),
                dma((4,)),
                dma((4,)),
                dma((3,)),
                dma((3,)),
                dma((3,)),
                dma((3,)),
            ],
            compiler_params=pltpu.CompilerParams(
                collective_id=0,
                has_side_effects=True,
                vmem_limit_bytes=40 * 1024 * 1024,
            ),
        )(
            pinned(positions.reshape(3, cells, TILE)),
            pinned(velocities.reshape(3, cells, TILE)),
            pinned(strength.reshape(cells, TILE)),
            pinned(tiles),
            pinned(plan.reshape(1, walkers)),
            pinned(plan),
            pinned(home),
            weights,
        )
        return (
            dist,
            npos.reshape(1, 3, cells * TILE),
            nvel.reshape(1, 3, cells * TILE),
            nwt.reshape(1),
        )

    return jax.shard_map(
        shards,
        mesh=mesh,
        in_specs=(
            P("walker", None, "space"),
            P("walker", None, "space"),
            P("walker"),
            P("space"),
            P("space", None),
            P(),
            P(),
        ),
        out_specs=(
            P("walker", "space"),
            P("walker", None, "space"),
            P("walker", None, "space"),
            P("walker"),
        ),
        check_vma=False,
    )
```
